32 devices in a mesh: expert: 4 (over x, core), latent: 8 (over z, y).
Axes of the slice: x: 2, y: 2, z: 4, core: 2. Of those that a mesh axis runs over, the one named last changes fastest.
Arguments:
- tokens: bfloat16 [256, 2560], P(('expert', 'latent')), may hold values from -6 to 6
- route: int32 [256, 1], P(('expert', 'latent')), may hold values from 0 to 3; in each aligned block of 8 rows (0 to 7, 8 to 15, ...) at most 2 rows name the same one
- blocks: int32 [256, 64], P(('expert', 'latent')), may hold values from 0 to 63, all different within a row
- weight: bfloat16 [4, 2560, 8192], P('expert', None, 'latent'), may hold values from -0.125 to 0.125
- enc_bias: float32 [4, 8192], P('expert', 'latent'), may hold values from -3 to 3
- dec_bias: float32 [2560], replicated, may hold values from -3 to 3
Outputs:
- grad_weight: bfloat16 [4, 2560, 8192], P('expert', None, 'latent')
- grad_enc: float32 [4, 8192], P('expert', 'latent')
- grad_dec: float32 [2560], replicated
- loss: float32 [], replicated
The draws below stay inside these ranges and needn't reach their ends.
Inputs may be any that keep to these rules, and one draw needn't show every extreme that they name: `route`: within the rows of one device (aligned blocks of 8 rows) no expert is named by more than 2 rows. Each row lists 64 different blocks.
All inputs are finite; a program needn't handle non-finite values.
Results may differ from the reference program's by a relative error of at most 0.012.
The reference program's roundings to bfloat16 on the way count: a program that leaves them out, or rounds other values in their place, can miss the bound.
Values may be sent and summed in bfloat16 or wider, within the bound.
A program may use at most 128 MiB of HBM per device.

```python
import math
import jax
import jax.numpy as jnp
import numpy as np
from jax import lax

D = 2560
BLK = 128
K = 64
TOK_DEV = 8
CAP = 2
EXPERTS = 4
LATENTS = 8192
TOKENS = 256


def levels(own_key, dims, pieces, least, largest):
    def one(axis_at, shards_of):
        heights = jax.random.uniform(jax.random.fold_in(jax.random.fold_in(own_key, 6), axis_at), (shards_of,), jnp.float32, least / len(pieces), largest / len(pieces))
        return jnp.repeat(jnp.exp(heights), dims[axis_at] // shards_of).reshape((-1,) + (1,) * (len(dims) - axis_at - 1))

    level = one(*pieces[0])
    for cut in pieces[1:]:
        level = level * one(*cut)
    return level


def picks_of(key, rows, count, top, lift):
    sequence = jax.random.permutation(jax.random.fold_in(key, 1), count)
    pull = sequence
    for power in range(3):
        pull = pull * pull // count
    pull = pull * lift // count
    tickets = jax.random.randint(jax.random.fold_in(key, 2), (rows, count), 0, 4096) + pull
    sure = jax.random.permutation(jax.random.fold_in(key, 3), rows)[jnp.arange(count) % rows]
    tickets = jnp.where(jnp.arange(rows)[:, None] == sure[None, :], 1 << 14, tickets)
    score = tickets * count + jnp.arange(count)
    return lax.top_k(score.astype(jnp.int32), top)[1].astype(jnp.int32)


def routed_block(rng, own, number, rows, amount, top, limit, lean):
    order = jax.random.permutation(rng, amount)
    heavy_load, common = portions_of(amount, rows * top, limit, lean, True), portions_of(amount, rows * top, limit, lean, False)
    places = jnp.arange(amount)

    def named(tallies, turn):
        used = int((tallies > 0).sum())
        fixed = max(1, used // 4)
        moved = fixed + (places - fixed + turn * (used - fixed)) % max(1, amount - fixed)
        return jnp.zeros((amount,), jnp.int32).at[order[jnp.where(places < fixed, places, moved)]].set(jnp.asarray(tallies, jnp.int32))

    tallies = jnp.where(number % 4 == 0, named(heavy_load, number // 4), named(common, number - number // 4 - 1))
    mixed = jax.random.permutation(jax.random.fold_in(own, 3), amount)
    source_of, taker = mixed[0:amount // 2 * 2:2], mixed[1:amount // 2 * 2:2]
    margin = jnp.minimum(tallies[source_of] - 1, limit - tallies[taker]) // 2
    margin = jnp.where((source_of == order[0]) | (taker == order[0]) | (tallies[taker] == 0), 0, jnp.maximum(margin, 0))
    moved = jax.random.randint(jax.random.fold_in(own, 4), (amount // 2,), 0, 1 << 20) % (margin + 1)
    tallies = tallies.at[source_of].add(-moved).at[taker].add(moved)
    labels = jnp.searchsorted(jnp.cumsum(tallies), jnp.arange(rows * top), side="right").astype(jnp.int32)
    listing = labels.reshape(top, rows).T
    listing = listing[jax.random.permutation(jax.random.fold_in(own, 1), rows)]
    turn = jax.random.randint(jax.random.fold_in(own, 2), (rows, 1), 0, top)
    return jnp.take_along_axis(listing, (jnp.arange(top)[None, :] + turn) % top, axis=1)


def portions_of(count, total, most, skew, full):
    portions = [(1 << 20) // math.isqrt(standing ** skew) + 1 for standing in range(1, count + 1)]
    largest = most if full else min(most, max(-(-total // count), total * portions[0] // sum(portions)))
    least = 1 if total - largest >= count - 1 else 0
    counts, rest = [largest] + [least] * (count - 1), total - largest - least * (count - 1)
    while rest > 0:
        movable = [i for i in range(1, count) if counts[i] < largest] or [i for i in range(1, count) if counts[i] < most]
        pool, budget = sum([portions[i] for i in movable]), rest
        for i in movable:
            extra = min(most - counts[i], max(1, budget * portions[i] // pool), rest)
            counts[i] = counts[i] + extra
            rest = rest - extra
    return np.array(counts)


def scatter_about(rng, extent, spread, limit, cuts=(), kind=jnp.bfloat16):
    level = levels(rng, extent, cuts, -0.22, 0.18) if cuts else 1.0
    values = jax.random.normal(rng, extent, jnp.float32) * spread * level
    return jnp.minimum(jnp.maximum(values, -limit), limit).astype(kind)


def setup_inputs(seed: int = 0) -> dict:
    arg_keys = jax.random.split(jax.random.key(seed), 7)
    tokens = scatter_about(arg_keys[0], (TOKENS, D), 1.0, 6.0, ((0, 32),))
    route_keys = jax.random.split(jax.random.fold_in(arg_keys[1], 1), TOKENS // TOK_DEV)
    route_turns = jax.random.permutation(jax.random.fold_in(arg_keys[1], 3), TOKENS // TOK_DEV)
    route = jax.vmap(lambda own, number: routed_block(jax.random.fold_in(arg_keys[1], 2), own, number, TOK_DEV, EXPERTS, 1, CAP, 2))(route_keys, route_turns).reshape((TOKENS, 1))
    blocks = picks_of(arg_keys[2], TOKENS, LATENTS // BLK, K, 8192)
    weight = scatter_about(arg_keys[3], (EXPERTS, D, LATENTS), D ** -0.5, 0.125, ((0, 4), (2, 8)))
    enc_bias = scatter_about(arg_keys[4], (EXPERTS, LATENTS), 0.5, 3.0, ((0, 4), (1, 8)), jnp.float32)
    dec_bias = scatter_about(arg_keys[5], (D,), 0.5, 3.0, (), jnp.float32)
    return {"tokens": tokens, "route": route, "blocks": blocks, "weight": weight, "enc_bias": enc_bias, "dec_bias": dec_bias}


def expert_table(route):
    sources = TOKENS // TOK_DEV
    expert_of = route[:, 0].astype(jnp.int32).reshape(sources, TOK_DEV)
    one_hot = (expert_of[:, :, None] == jnp.arange(EXPERTS, dtype=jnp.int32)[None, None, :]).astype(jnp.int32)
    earlier = jnp.sum((jnp.cumsum(one_hot, axis=1) - one_hot) * one_hot, axis=2).astype(jnp.int32)
    position = (jnp.arange(sources, dtype=jnp.int32)[:, None] * CAP + earlier).astype(jnp.int32)
    token_ids = jnp.arange(TOKENS, dtype=jnp.int32).reshape(sources, TOK_DEV)
    table = jnp.full((EXPERTS, sources * CAP), -1, jnp.int32)
    return table.at[expert_of.reshape(-1), position.reshape(-1)].set(token_ids.reshape(-1))


def reference(tokens, route, blocks, weight, enc_bias, dec_bias):
    table = expert_table(route)
    block_count = LATENTS // BLK

    def one_expert(operands):
        token_ids, weights_here, bias_here = operands
        valid = (token_ids >= 0).astype(jnp.float32)
        safe_ids = jnp.maximum(token_ids, 0).astype(jnp.int32)
        rows_f32 = tokens[safe_ids].astype(jnp.float32) * valid[:, None]
        listed = blocks[safe_ids]
        chosen = jnp.any(listed[:, :, None] == jnp.arange(block_count, dtype=jnp.int32)[None, None, :], axis=1)
        mask = jnp.repeat(chosen.astype(jnp.float32) * valid[:, None], BLK, axis=1)
        shifted = (rows_f32 - dec_bias).astype(jnp.bfloat16)
        pre_act = jnp.dot(shifted, weights_here, preferred_element_type=jnp.float32) + bias_here
        active = jnp.maximum(pre_act, 0.0) * mask
        active_bf = active.astype(jnp.bfloat16)
        recon = jnp.dot(active_bf, weights_here.T, preferred_element_type=jnp.float32) + dec_bias
        error = (recon - rows_f32) * valid[:, None]
        error_bf = error.astype(jnp.bfloat16)
        grad_act = jnp.dot(error_bf, weights_here, preferred_element_type=jnp.float32)
        grad_pre = grad_act * (pre_act > 0.0).astype(jnp.float32) * mask
        grad_pre_bf = grad_pre.astype(jnp.bfloat16)
        grad_here = jnp.dot(shifted.T, grad_pre_bf, preferred_element_type=jnp.float32)
        grad_here = grad_here + jnp.dot(error_bf.T, active_bf, preferred_element_type=jnp.float32)
        grad_bias = jnp.sum(grad_pre, axis=0)
        pulled = jnp.dot(weights_here, grad_bias.astype(jnp.bfloat16), preferred_element_type=jnp.float32)
        return grad_here.astype(jnp.bfloat16), grad_bias, jnp.sum(error, axis=0) - pulled, 0.5 * jnp.sum(error * error)

    grad_weight, grad_enc, dec_terms, loss_terms = lax.map(one_expert, (table, weight, enc_bias))
    grad_dec = jnp.sum(dec_terms, axis=0)
    loss = jnp.sum(loss_terms) / TOKENS
    return (grad_weight, grad_enc, grad_dec, loss)
```

```python
import functools
import jax
import jax.numpy as jnp
from jax import lax
from jax.experimental import pallas as pl
from jax.experimental.pallas import tpu as pltpu
from jax.sharding import PartitionSpec as P

BLK = 128
CAP = 2
PACK = 16
PARTS = PACK // CAP
LANES = 128
TILE = 256
MESH = pl.DeviceIdType.MESH
ALONG_LAST = (((1,), (1,)), ((), ()))
ALONG_FIRST = (((0,), (0,)), ((), ()))


def step_kernel(
    n_e, n_l, n_tok, width, list_len,
    tok_ref, route_ref, blocks_ref, w_hbm, encb_ref, decb_ref,
    left_ref, right_ref, genc_ref, gdec_ref, loss_ref,
    w_ref, aug, pack, mine, gathered, rows, shifted, gate, part, rs_send, rs_recv, ag_recv, err, vec_e, vec_l,
    w_sem, s1, r1, s2, r2, s3, r3, s4, r4, s5, r5, s6, r6,
):
    me_e = lax.axis_index("expert")
    me_l = lax.axis_index("latent")
    share = n_e * CAP
    count = n_l * share
    half = width // 2
    chunk = aug.shape[1] // PARTS
    latents = w_ref.shape[1]

    def to_expert(src, dst, ssem, rsem, peer, slot):
        return pltpu.make_async_remote_copy(
            src_ref=src, dst_ref=dst, send_sem=ssem.at[peer], recv_sem=rsem.at[slot],
            device_id=(peer, me_l), device_id_type=MESH)

    def to_latent(src, dst, ssem, rsem, peer, slot):
        return pltpu.make_async_remote_copy(
            src_ref=src, dst_ref=dst, send_sem=ssem.at[peer], recv_sem=rsem.at[slot],
            device_id=(me_e, peer), device_id_type=MESH)

    def peers(me, n):
        return [lax.rem(me + k, n) for k in range(1, n)]

    w_copy = pltpu.make_async_copy(w_hbm.at[0], w_ref, w_sem)
    w_copy.start()
    barrier = pltpu.get_barrier_semaphore()
    for p in peers(me_e, n_e):
        pl.semaphore_signal(barrier, inc=1, device_id=(p, me_l), device_id_type=MESH)
    for p in peers(me_l, n_l):
        pl.semaphore_signal(barrier, inc=1, device_id=(me_e, p), device_id_type=MESH)

    aug[...] = jnp.zeros_like(aug)
    aug[:, :width] = tok_ref[...].astype(jnp.float32)
    aug[:, width:width + list_len] = (blocks_ref[...] + 1).astype(jnp.float32)
    route = route_ref[...]
    one_hot = (route == lax.broadcasted_iota(jnp.int32, (n_tok, LANES), 1)).astype(jnp.float32)
    before = (lax.broadcasted_iota(jnp.int32, (n_tok, n_tok), 1)
              < lax.broadcasted_iota(jnp.int32, (n_tok, n_tok), 0)).astype(jnp.float32)
    earlier = jnp.sum(jnp.dot(before, one_hot, preferred_element_type=jnp.float32) * one_hot, axis=1, keepdims=True)
    target = route.astype(jnp.float32) * CAP + earlier
    target = jnp.concatenate([target] * PARTS, axis=0)
    stacked = jnp.concatenate([aug[:, c * chunk:(c + 1) * chunk] for c in range(PARTS)], axis=0).astype(jnp.bfloat16)
    shape = (PARTS * n_tok, n_e * PACK)
    row = lax.broadcasted_iota(jnp.int32, shape, 0)
    col = lax.broadcasted_iota(jnp.int32, shape, 1)
    place = (col >> 4) * CAP + (col & 1)
    hit = (target == place.astype(jnp.float32)) & ((row >> 3) == ((col >> 1) & (PARTS - 1)))
    packed = lax.dot_general(hit.astype(jnp.bfloat16), stacked, ALONG_FIRST, preferred_element_type=jnp.float32)
    pack[...] = packed.astype(jnp.bfloat16).reshape(pack.shape)

    pl.semaphore_wait(barrier, (n_e - 1) + (n_l - 1))
    for p in peers(me_e, n_e):
        to_expert(pack.at[p], mine.at[me_e], s1, r1, p, me_e).start()
    mine[me_e] = pack[me_e]
    for p in peers(me_e, n_e):
        to_expert(pack.at[p], mine.at[p], s1, r1, p, p).wait_recv()
    for p in peers(me_l, n_l):
        to_latent(mine, gathered.at[me_l], s2, r2, p, me_l).start()

    shape = (n_e * PACK, n_e * PACK)
    row = lax.broadcasted_iota(jnp.int32, shape, 0)
    col = lax.broadcasted_iota(jnp.int32, shape, 1)
    unpack = (row == ((col >> 1) & (PARTS - 1)) * share + (col >> 4) * CAP + (col & 1)).astype(jnp.bfloat16)

    def place_rows(source, block):
        flat = jnp.dot(unpack, block.reshape(n_e * PACK, chunk), preferred_element_type=jnp.float32)
        at = pl.ds(pl.multiple_of(source * share, 8), share)
        for c in range(rows.shape[1] // chunk):
            rows[at, c * chunk:(c + 1) * chunk] = flat[c * share:(c + 1) * share]

    place_rows(me_l, mine[...])

    @pl.loop(1, n_l)
    def _(k):
        p = lax.rem(me_l + k, n_l)
        to_latent(mine, gathered.at[p], s2, r2, p, p).wait_recv()
        place_rows(p, gathered[p])

    decb = decb_ref[...]
    bf = (rows[:, :width] - decb).astype(jnp.bfloat16)
    shifted[...] = bf
    left_ref[:count, :] = bf
    lists = rows[:, width:width + LANES]
    first_block = me_l * (latents // BLK)
    for b in range(latents // BLK):
        number = (first_block + b + 1).astype(jnp.float32)
        found = jnp.max((lists == number).astype(jnp.float32), axis=1, keepdims=True)
        gate[:, b * BLK:(b + 1) * BLK] = jnp.broadcast_to(found, (count, BLK))

    w_copy.wait()

    @pl.loop(0, latents // TILE)
    def _(j):
        at = pl.ds(pl.multiple_of(j * TILE, TILE), TILE)
        pre = jnp.dot(shifted[...], w_ref[:, at], preferred_element_type=jnp.float32) + encb_ref[:, at]
        mask = gate[:, at]
        right_ref[count:, at] = (jnp.maximum(pre, 0.0) * mask).astype(jnp.bfloat16)
        gate[:, at] = jnp.where(pre > 0.0, mask, 0.0)

    @pl.loop(0, width // TILE)
    def _(j):
        at = pl.ds(pl.multiple_of(j * TILE, TILE), TILE)
        part[:, at] = lax.dot_general(
            right_ref[count:, :], w_ref[at, :], ALONG_LAST, preferred_element_type=jnp.float32)

    def folded(value):
        return jnp.concatenate([value[:, :half], value[:, half:]], axis=0)

    @pl.loop(1, n_l)
    def _(k):
        p = lax.rem(me_l + k, n_l)
        rs_send[p] = folded(part[pl.ds(pl.multiple_of(p * share, 8), share), :]).astype(jnp.bfloat16)
        to_latent(rs_send.at[p], rs_recv.at[me_l], s3, r3, p, me_l).start()

    own = pl.ds(pl.multiple_of(me_l * share, 8), share)
    rs_recv[me_l] = folded(part[own, :]).astype(jnp.bfloat16)
    for p in peers(me_l, n_l):
        to_latent(rs_send.at[p], rs_recv.at[p], s3, r3, p, p).wait_recv()
    total = jnp.zeros((2 * share, half), jnp.float32)
    for s in range(n_l):
        total = total + rs_recv[s].astype(jnp.float32)
    recon = jnp.concatenate([total[:share], total[share:]], axis=1) + decb
    valid = (rows[own, width:width + 1] > 0.5).astype(jnp.float32)
    error = (recon - rows[own, :width]) * valid
    ag_recv[me_l] = folded(error).astype(jnp.bfloat16)
    for p in peers(me_l, n_l):
        to_latent(ag_recv.at[me_l], ag_recv.at[me_l], s4, r4, p, me_l).start()
    error_sum = jnp.sum(error, axis=0, keepdims=True)
    loss = 0.5 * jnp.sum(error * error)
    for p in peers(me_l, n_l):
        to_latent(ag_recv.at[p], ag_recv.at[p], s4, r4, p, p).wait_recv()

    @pl.loop(0, n_l)
    def _(s):
        got = ag_recv[s].astype(jnp.float32)
        at = pl.ds(pl.multiple_of(s * share, 8), share)
        err[at, :half] = got[:share]
        err[at, half:] = got[share:]

    left_ref[count:, :] = err[...].astype(jnp.bfloat16)

    @pl.loop(0, latents // TILE)
    def _(j):
        at = pl.ds(pl.multiple_of(j * TILE, TILE), TILE)
        grad = jnp.dot(left_ref[count:, :], w_ref[:, at], preferred_element_type=jnp.float32) * gate[:, at]
        right_ref[:count, at] = grad.astype(jnp.bfloat16)
        genc_ref[:, at] = jnp.sum(grad, axis=0, keepdims=True)

    column = jnp.broadcast_to(genc_ref[...], (8, latents)).astype(jnp.bfloat16)
    for j in range(width // TILE):
        at = slice(j * TILE, (j + 1) * TILE)
        pulled = lax.dot_general(column, w_ref[at, :], ALONG_LAST, preferred_element_type=jnp.float32)
        vec_e[me_e, :, at] = error_sum[:, at] - pulled[:1]
    vec_e[me_e, :, width:] = jnp.broadcast_to(loss.reshape(1, 1), (1, LANES))

    for p in peers(me_e, n_e):
        to_expert(vec_e.at[me_e], vec_e.at[me_e], s5, r5, p, me_e).start()
    for p in peers(me_e, n_e):
        to_expert(vec_e.at[p], vec_e.at[p], s5, r5, p, p).wait_recv()
    vec = vec_e[0]
    for s in range(1, n_e):
        vec = vec + vec_e[s]
    vec_l[me_l] = vec
    for p in peers(me_l, n_l):
        to_latent(vec_l.at[me_l], vec_l.at[me_l], s6, r6, p, me_l).start()
    for p in peers(me_l, n_l):
        to_latent(vec_l.at[p], vec_l.at[p], s6, r6, p, p).wait_recv()
    vec = vec_l[0]
    for s in range(1, n_l):
        vec = vec + vec_l[s]
    gdec_ref[...] = vec[:, :width]
    loss_ref[...] = vec[:, width:] * (1.0 / (n_tok * n_e * n_l))

    for p in peers(me_e, n_e):
        to_expert(pack.at[p], mine.at[me_e], s1, r1, p, me_e).wait_send()
        to_expert(vec_e.at[me_e], vec_e.at[me_e], s5, r5, p, me_e).wait_send()
    for p in peers(me_l, n_l):
        to_latent(mine, gathered.at[me_l], s2, r2, p, me_l).wait_send()
        to_latent(rs_send.at[p], rs_recv.at[me_l], s3, r3, p, me_l).wait_send()
        to_latent(ag_recv.at[me_l], ag_recv.at[me_l], s4, r4, p, me_l).wait_send()
        to_latent(vec_l.at[me_l], vec_l.at[me_l], s6, r6, p, me_l).wait_send()


def shards(tokens, route, blocks, weight, enc_bias, dec_bias):
    n_e = lax.axis_size("expert")
    n_l = lax.axis_size("latent")
    n_tok, width = tokens.shape
    list_len = blocks.shape[1]
    latents = weight.shape[2]
    share = n_e * CAP
    count = n_l * share
    aug_width = -(-(width + LANES) // (PARTS * LANES)) * PARTS * LANES
    chunk = aug_width // PARTS
    row_width = -(-(width + LANES) // chunk) * chunk
    vmem = pl.BlockSpec(memory_space=pltpu.VMEM)
    dma = pltpu.SemaphoreType.DMA
    f32, bf16 = jnp.float32, jnp.bfloat16
    left, right, genc, gdec, loss = pl.pallas_call(
        functools.partial(step_kernel, n_e, n_l, n_tok, width, list_len),
        out_shape=(
            jax.ShapeDtypeStruct((2 * count, width), bf16),
            jax.ShapeDtypeStruct((2 * count, latents), bf16),
            jax.ShapeDtypeStruct((1, latents), f32),
            jax.ShapeDtypeStruct((1, width), f32),
            jax.ShapeDtypeStruct((1, LANES), f32),
        ),
        in_specs=[vmem, vmem, vmem, pl.BlockSpec(memory_space=pl.ANY), vmem, vmem],
        out_specs=[vmem] * 5,
        scratch_shapes=[
            pltpu.VMEM((width, latents), bf16),
            pltpu.VMEM((n_tok, aug_width), f32),
            pltpu.VMEM((n_e, PACK, chunk), bf16),
            pltpu.VMEM((n_e, PACK, chunk), bf16),
            pltpu.VMEM((n_l, n_e, PACK, chunk), bf16),
            pltpu.VMEM((count, row_width), f32),
            pltpu.VMEM((count, width), bf16),
            pltpu.VMEM((count, latents), f32),
            pltpu.VMEM((count, width), f32),
            pltpu.VMEM((n_l, 2 * share, width // 2), bf16),
            pltpu.VMEM((n_l, 2 * share, width // 2), bf16),
            pltpu.VMEM((n_l, 2 * share, width // 2), bf16),
            pltpu.VMEM((count, width), f32),
            pltpu.VMEM((n_e, 1, width + LANES), f32),
            pltpu.VMEM((n_l, 1, width + LANES), f32),
            dma,
            dma((n_e,)), dma((n_e,)),
            dma((n_l,)), dma((n_l,)),
            dma((n_l,)), dma((n_l,)),
            dma((n_l,)), dma((n_l,)),
            dma((n_e,)), dma((n_e,)),
            dma((n_l,)), dma((n_l,)),
        ],
        compiler_params=pltpu.CompilerParams(
            collective_id=0, has_side_effects=True, vmem_limit_bytes=56 << 20),
        name="sae_step",
    )(tokens, route, blocks, weight, enc_bias, dec_bias[None])
    grad = lax.dot_general(left, right, ALONG_FIRST, preferred_element_type=f32)
    return grad.astype(bf16)[None], genc, gdec[0], loss[0, 0]


def solution(mesh):
    return jax.shard_map(
        shards,
        mesh=mesh,
        in_specs=(
            P(("expert", "latent"), None),
            P(("expert", "latent"), None),
            P(("expert", "latent"), None),
            P("expert", None, "latent"),
            P("expert", "latent"),
            P(),
        ),
        out_specs=(P("expert", None, "latent"), P("expert", "latent"), P(), P()),
        check_vma=False,
    )
```

```python
import functools
import jax
import jax.numpy as jnp
from jax import lax
from jax.experimental import pallas as pl
from jax.experimental.pallas import tpu as pltpu
from jax.sharding import PartitionSpec as P

BLK = 128
CAP = 2
PACK = 16
PARTS = PACK // CAP
LANES = 128
TILE = 256
MESH = pl.DeviceIdType.MESH
ALONG_LAST = (((1,), (1,)), ((), ()))
ALONG_FIRST = (((0,), (0,)), ((), ()))


def step_kernel(
    n_e, n_l, n_tok, width, list_len,
    tok_ref, route_ref, blocks_ref, w_hbm, encb_ref, decb_ref,
    left_ref, right_ref, genc_ref, gdec_ref, loss_ref,
    w_ref, aug, pack, mine, gathered, rows, shifted, gate, part, rs_send, rs_recv, ag_recv, err, acc, vec_e, vec_l,
    w_sem, s1, r1, s2, r2, s3, r3, s4, r4, s5, r5, s6, r6,
):
    me_e = lax.axis_index("expert")
    me_l = lax.axis_index("latent")
    share = n_e * CAP
    count = n_l * share
    half = width // 2
    quarter = half // 2
    chunk = aug.shape[1] // PARTS
    latents = w_ref.shape[1]

    def to_expert(src, dst, ssem, rsem, peer, slot):
        return pltpu.make_async_remote_copy(
            src_ref=src, dst_ref=dst, send_sem=ssem.at[peer], recv_sem=rsem.at[slot],
            device_id=(peer, me_l), device_id_type=MESH)

    def to_latent(src, dst, ssem, rsem, peer, slot):
        return pltpu.make_async_remote_copy(
            src_ref=src, dst_ref=dst, send_sem=ssem.at[peer], recv_sem=rsem.at[slot],
            device_id=(me_e, peer), device_id_type=MESH)

    def peers(me, n):
        return [lax.rem(me + k, n) for k in range(1, n)]

    partner = me_l + 1 - 2 * lax.rem(me_l, 2)
    alike = [lax.rem(me_l + 2 * k, n_l) for k in range(1, n_l // 2)]

    def spread(src, dst, ssem, rsem):
        for p in alike + [partner]:
            to_latent(src, dst.at[me_l], ssem, rsem, p, me_l).start()

    def collect(dst, ssem, rsem, use):
        @pl.loop(1, n_l // 2)
        def _(k):
            p = lax.rem(me_l + 2 * k, n_l)
            to_latent(dst.at[p], dst.at[p], ssem, rsem, p, p).wait_recv()
            pltpu.make_async_remote_copy(
                src_ref=dst.at[p], dst_ref=dst.at[p], send_sem=ssem.at[n_l + p], recv_sem=rsem.at[p],
                device_id=(me_e, partner), device_id_type=MESH).start()
            use(p)

        @pl.loop(0, n_l // 2)
        def _(k):
            p = lax.rem(partner + 2 * k, n_l)
            to_latent(dst.at[p], dst.at[p], ssem, rsem, p, p).wait_recv()
            use(p)

    def drain(src, dst, ssem, rsem):
        for p in alike + [partner]:
            to_latent(src, dst.at[me_l], ssem, rsem, p, me_l).wait_send()
        for p in alike:
            pltpu.make_async_remote_copy(
                src_ref=dst.at[p], dst_ref=dst.at[p], send_sem=ssem.at[n_l + p], recv_sem=rsem.at[p],
                device_id=(me_e, partner), device_id_type=MESH).wait_send()

    w_copy = pltpu.make_async_copy(w_hbm.at[0], w_ref, w_sem)
    w_copy.start()
    barrier = pltpu.get_barrier_semaphore()
    for p in peers(me_e, n_e):
        pl.semaphore_signal(barrier, inc=1, device_id=(p, me_l), device_id_type=MESH)
    for p in peers(me_l, n_l):
        pl.semaphore_signal(barrier, inc=1, device_id=(me_e, p), device_id_type=MESH)

    aug[...] = jnp.zeros_like(aug)
    aug[:, :width] = tok_ref[...].astype(jnp.float32)
    aug[:, width:width + list_len] = (blocks_ref[...] + 1).astype(jnp.float32)
    route = jnp.broadcast_to(route_ref[...], (8, n_tok))
    one_hot = (route == lax.broadcasted_iota(jnp.int32, (8, n_tok), 0)).astype(jnp.float32)
    before = (lax.broadcasted_iota(jnp.int32, (n_tok, n_tok), 0)
              < lax.broadcasted_iota(jnp.int32, (n_tok, n_tok), 1)).astype(jnp.float32)
    earlier = jnp.sum(jnp.dot(one_hot, before, preferred_element_type=jnp.float32) * one_hot, axis=0, keepdims=True)
    target = (route.astype(jnp.float32) * CAP + earlier).astype(jnp.bfloat16)
    repeat = (lax.broadcasted_iota(jnp.int32, (n_tok, PARTS * n_tok), 0)
              == (lax.broadcasted_iota(jnp.int32, (n_tok, PARTS * n_tok), 1) & (n_tok - 1))).astype(jnp.bfloat16)
    target = jnp.dot(target, repeat, preferred_element_type=jnp.float32)[:1]
    stacked = jnp.concatenate([aug[:, c * chunk:(c + 1) * chunk] for c in range(PARTS)], axis=0).astype(jnp.bfloat16)
    shape = (n_e * PACK, PARTS * n_tok)
    row = lax.broadcasted_iota(jnp.int32, shape, 0)
    col = lax.broadcasted_iota(jnp.int32, shape, 1)
    place = (row >> 4) * CAP + (row & 1)
    hit = (target == place.astype(jnp.float32)) & (col // n_tok == ((row >> 1) & (PARTS - 1)))
    packed = jnp.dot(hit.astype(jnp.bfloat16), stacked, preferred_element_type=jnp.float32)
    pack[...] = packed.astype(jnp.bfloat16).reshape(pack.shape)

    pl.semaphore_wait(barrier, (n_e - 1) + (n_l - 1))
    for p in peers(me_e, n_e):
        to_expert(pack.at[p], mine.at[me_e], s1, r1, p, me_e).start()
    mine[me_e] = pack[me_e]
    for p in peers(me_e, n_e):
        to_expert(pack.at[p], mine.at[p], s1, r1, p, p).wait_recv()
    spread(mine, gathered, s2, r2)

    shape = (n_e * PACK, n_e * PACK)
    row = lax.broadcasted_iota(jnp.int32, shape, 0)
    col = lax.broadcasted_iota(jnp.int32, shape, 1)
    unpack = (row == ((col >> 1) & (PARTS - 1)) * share + (col >> 4) * CAP + (col & 1)).astype(jnp.bfloat16)

    def place_rows(source, block):
        flat = jnp.dot(unpack, block.reshape(n_e * PACK, chunk), preferred_element_type=jnp.float32)
        at = pl.ds(pl.multiple_of(source * share, 8), share)
        for c in range(rows.shape[1] // chunk):
            rows[at, c * chunk:(c + 1) * chunk] = flat[c * share:(c + 1) * share]

    place_rows(me_l, mine[...])

    collect(gathered, s2, r2, lambda p: place_rows(p, gathered[p]))

    decb = decb_ref[...].reshape(1, width)
    bf = (rows[:, :width] - decb).astype(jnp.bfloat16)
    shifted[...] = bf
    left_ref[:count, :] = bf
    lists = rows[:, width:width + LANES]
    first_block = me_l * (latents // BLK)
    for b in range(latents // BLK):
        number = (first_block + b + 1).astype(jnp.float32)
        found = jnp.max((lists == number).astype(jnp.float32), axis=1, keepdims=True)
        gate[:, b * BLK:(b + 1) * BLK] = jnp.broadcast_to(found, (count, BLK))

    w_copy.wait()

    @pl.loop(0, latents // TILE)
    def _(j):
        at = pl.ds(pl.multiple_of(j * TILE, TILE), TILE)
        pre = jnp.dot(shifted[...], w_ref[:, at], preferred_element_type=jnp.float32) + encb_ref[:, at]
        mask = gate[:, at]
        right_ref[count:, at] = (jnp.maximum(pre, 0.0) * mask).astype(jnp.bfloat16)
        gate[:, at] = jnp.where(pre > 0.0, mask, 0.0)

    def folded(value):
        return jnp.concatenate([value[:, :quarter], value[:, quarter:]], axis=0)

    def unfolded(value):
        return jnp.concatenate([value[:share], value[share:]], axis=1)

    own = pl.ds(pl.multiple_of(me_l * share, 8), share)
    for h in range(2):
        @pl.loop(0, half // TILE)
        def _(j):
            at = pl.ds(pl.multiple_of(h * half + j * TILE, TILE), TILE)
            part[:, at] = lax.dot_general(
                right_ref[count:, :], w_ref[at, :], ALONG_LAST, preferred_element_type=jnp.float32)

        cols = slice(h * half, (h + 1) * half)

        @pl.loop(1, n_l)
        def _(k):
            p = lax.rem(me_l + k, n_l)
            rs_send[h, p] = folded(part[pl.ds(pl.multiple_of(p * share, 8), share), cols]).astype(jnp.bfloat16)
            to_latent(rs_send.at[h, p], rs_recv.at[h, me_l], s3.at[h], r3.at[h], p, me_l).start()

    valid = (rows[own, width:width + 1] > 0.5).astype(jnp.float32)
    loss = jnp.zeros((), jnp.float32)
    error_sum = []
    for h in range(2):
        cols = slice(h * half, (h + 1) * half)
        total = part[own, cols]
        for p in peers(me_l, n_l):
            to_latent(rs_send.at[h, p], rs_recv.at[h, p], s3.at[h], r3.at[h], p, p).wait_recv()
            total = total + unfolded(rs_recv[h, p].astype(jnp.float32))
        error = (total + decb[:, cols] - rows[own, cols]) * valid
        ag_recv[h, me_l] = folded(error).astype(jnp.bfloat16)
        spread(ag_recv.at[h, me_l], ag_recv.at[h], s4.at[h], r4.at[h])
        error_sum.append(jnp.sum(error, axis=0, keepdims=True))
        loss = loss + 0.5 * jnp.sum(error * error)
    error_sum = jnp.concatenate(error_sum, axis=1)

    for h in range(2):
        cols = slice(h * half, (h + 1) * half)

        def place_error(s):
            at = pl.ds(pl.multiple_of(s * share, 8), share)
            err[at, :] = unfolded(ag_recv[h, s].astype(jnp.float32))

        place_error(me_l)
        collect(ag_recv.at[h], s4.at[h], r4.at[h], place_error)
        left_ref[count:, cols] = err[...].astype(jnp.bfloat16)

        @pl.loop(0, latents // TILE)
        def _(j):
            at = pl.ds(pl.multiple_of(j * TILE, TILE), TILE)
            grad = jnp.dot(left_ref[count:, cols], w_ref[cols, at], preferred_element_type=jnp.float32)
            if h == 0:
                acc[:, at] = grad
            else:
                grad = (acc[:, at] + grad) * gate[:, at]
                right_ref[:count, at] = grad.astype(jnp.bfloat16)
                genc_ref[:, at] = jnp.sum(grad, axis=0, keepdims=True)

    column = jnp.broadcast_to(genc_ref[...], (8, latents)).astype(jnp.bfloat16)
    for j in range(width // TILE):
        at = slice(j * TILE, (j + 1) * TILE)
        pulled = lax.dot_general(column, w_ref[at, :], ALONG_LAST, preferred_element_type=jnp.float32)
        vec_e[me_e, :, at] = error_sum[:, at] - pulled[:1]
    vec_e[me_e, :, width:] = jnp.broadcast_to(loss.reshape(1, 1), (1, LANES))

    for p in peers(me_e, n_e):
        to_expert(vec_e.at[me_e], vec_e.at[me_e], s5, r5, p, me_e).start()
    for p in peers(me_e, n_e):
        to_expert(vec_e.at[p], vec_e.at[p], s5, r5, p, p).wait_recv()
    vec = vec_e[0]
    for s in range(1, n_e):
        vec = vec + vec_e[s]
    vec_l[me_l] = vec
    for p in peers(me_l, n_l):
        to_latent(vec_l.at[me_l], vec_l.at[me_l], s6, r6, p, me_l).start()
    for p in peers(me_l, n_l):
        to_latent(vec_l.at[p], vec_l.at[p], s6, r6, p, p).wait_recv()
    vec = vec_l[0]
    for s in range(1, n_l):
        vec = vec + vec_l[s]
    gdec_ref[...] = vec[:, :width].reshape(width)
    loss_ref[0] = vec[0, width] * (1.0 / (n_tok * n_e * n_l))

    for p in peers(me_e, n_e):
        to_expert(pack.at[p], mine.at[me_e], s1, r1, p, me_e).wait_send()
        to_expert(vec_e.at[me_e], vec_e.at[me_e], s5, r5, p, me_e).wait_send()
    for p in peers(me_l, n_l):
        to_latent(vec_l.at[me_l], vec_l.at[me_l], s6, r6, p, me_l).wait_send()
    drain(mine, gathered, s2, r2)
    for h in range(2):
        drain(ag_recv.at[h, me_l], ag_recv.at[h], s4.at[h], r4.at[h])
        for p in peers(me_l, n_l):
            to_latent(rs_send.at[h, p], rs_recv.at[h, me_l], s3.at[h], r3.at[h], p, me_l).wait_send()


def grad_kernel(left_ref, right_ref, out_ref):
    out_ref[0] = lax.dot_general(
        left_ref[...], right_ref[...], ALONG_FIRST, preferred_element_type=jnp.float32).astype(out_ref.dtype)


def shards(tokens, route, blocks, weight, enc_bias, dec_bias):
    n_e = lax.axis_size("expert")
    n_l = lax.axis_size("latent")
    n_tok, width = tokens.shape
    list_len = blocks.shape[1]
    latents = weight.shape[2]
    share = n_e * CAP
    count = n_l * share
    aug_width = -(-(width + LANES) // (PARTS * LANES)) * PARTS * LANES
    chunk = aug_width // PARTS
    row_width = -(-(width + LANES) // chunk) * chunk
    vmem = pl.BlockSpec(memory_space=pltpu.VMEM)
    dma = pltpu.SemaphoreType.DMA
    f32, bf16 = jnp.float32, jnp.bfloat16
    left, right, genc, gdec, loss = pl.pallas_call(
        functools.partial(step_kernel, n_e, n_l, n_tok, width, list_len),
        out_shape=(
            jax.ShapeDtypeStruct((2 * count, width), bf16),
            jax.ShapeDtypeStruct((2 * count, latents), bf16),
            jax.ShapeDtypeStruct((1, latents), f32),
            jax.ShapeDtypeStruct((width,), f32),
            jax.ShapeDtypeStruct((1,), f32),
        ),
        in_specs=[vmem, vmem, vmem, pl.BlockSpec(memory_space=pl.ANY), vmem, vmem],
        out_specs=[vmem] * 4 + [pl.BlockSpec(memory_space=pltpu.SMEM)],
        scratch_shapes=[
            pltpu.VMEM((width, latents), bf16),
            pltpu.VMEM((n_tok, aug_width), f32),
            pltpu.VMEM((n_e, PACK, chunk), bf16),
            pltpu.VMEM((n_e, PACK, chunk), bf16),
            pltpu.VMEM((n_l, n_e, PACK, chunk), bf16),
            pltpu.VMEM((count, row_width), f32),
            pltpu.VMEM((count, width), bf16),
            pltpu.VMEM((count, latents), f32),
            pltpu.VMEM((count, width), f32),
            pltpu.VMEM((2, n_l, 2 * share, width // 4), bf16),
            pltpu.VMEM((2, n_l, 2 * share, width // 4), bf16),
            pltpu.VMEM((2, n_l, 2 * share, width // 4), bf16),
            pltpu.VMEM((count, width // 2), f32),
            pltpu.VMEM((count, latents), f32),
            pltpu.VMEM((n_e, 1, width + LANES), f32),
            pltpu.VMEM((n_l, 1, width + LANES), f32),
            dma,
            dma((n_e,)), dma((n_e,)),
            dma((2 * n_l,)), dma((n_l,)),
            dma((2, n_l)), dma((2, n_l)),
            dma((2, 2 * n_l)), dma((2, n_l)),
            dma((n_e,)), dma((n_e,)),
            dma((n_l,)), dma((n_l,)),
        ],
        compiler_params=pltpu.CompilerParams(
            collective_id=0, has_side_effects=True, vmem_limit_bytes=56 << 20),
        name="sae_step",
    )(tokens, route.reshape(1, n_tok), blocks, weight, enc_bias, dec_bias)
    strip = 2 * TILE
    grad = pl.pallas_call(
        grad_kernel,
        out_shape=jax.ShapeDtypeStruct((1, width, latents), bf16),
        grid=(width // strip,),
        in_specs=[
            pl.BlockSpec((2 * count, strip), lambda i: (0, i)),
            pl.BlockSpec((2 * count, latents), lambda i: (0, 0)),
        ],
        out_specs=pl.BlockSpec((1, strip, latents), lambda i: (0, i, 0)),
        compiler_params=pltpu.CompilerParams(vmem_limit_bytes=56 << 20),
        name="grad_weight",
    )(left, right)
    return grad, genc, gdec, loss[0]


def solution(mesh):
    return jax.shard_map(
        shards,
        mesh=mesh,
        in_specs=(
            P(("expert", "latent"), None),
            P(("expert", "latent"), None),
            P(("expert", "latent"), None),
            P("expert", None, "latent"),
            P("expert", "latent"),
            P(),
        ),
        out_specs=(P("expert", None, "latent"), P("expert", "latent"), P(), P()),
        check_vma=False,
    )
```

```python
import functools
import jax
import jax.numpy as jnp
from jax import lax
from jax.experimental import pallas as pl
from jax.experimental.pallas import tpu as pltpu
from jax.sharding import PartitionSpec as P

BLK = 128
CAP = 2
PACK = 16
PARTS = PACK // CAP
LANES = 128
TILE = 256
MESH = pl.DeviceIdType.MESH
ALONG_LAST = (((1,), (1,)), ((), ()))
ALONG_FIRST = (((0,), (0,)), ((), ()))


def step_kernel(
    n_e, n_l, n_tok, width, list_len,
    tok_ref, route_ref, blocks_ref, w_hbm, encb_ref, decb_ref,
    left_ref, right_ref, genc_ref, gdec_ref, loss_ref,
    w_ref, aug, pack, mine, gathered, rows, shifted, gate, part, rs_send, rs_recv, ag_recv, err, acc, vec_e, vec_l,
    w_sem, s1, r1, s2, r2, s3, r3, s4, r4, s5, r5, s6, r6,
):
    me_e = lax.axis_index("expert")
    me_l = lax.axis_index("latent")
    share = n_e * CAP
    count = n_l * share
    half = width // 2
    quarter = half // 2
    chunk = aug.shape[1] // PARTS
    latents = w_ref.shape[1]
    few = count <= LANES
    wide = latents if few else TILE
    deep = half if few else TILE

    def to_expert(src, dst, ssem, rsem, peer, slot):
        return pltpu.make_async_remote_copy(
            src_ref=src, dst_ref=dst, send_sem=ssem.at[peer], recv_sem=rsem.at[slot],
            device_id=(peer, me_l), device_id_type=MESH)

    def to_latent(src, dst, ssem, rsem, peer, slot):
        return pltpu.make_async_remote_copy(
            src_ref=src, dst_ref=dst, send_sem=ssem.at[peer], recv_sem=rsem.at[slot],
            device_id=(me_e, peer), device_id_type=MESH)

    def peers(me, n):
        return [lax.rem(me + k, n) for k in range(1, n)]

    partner = me_l + 1 - 2 * lax.rem(me_l, 2)
    alike = [lax.rem(me_l + 2 * k, n_l) for k in range(1, n_l // 2)]

    def spread(src, dst, ssem, rsem):
        for p in alike + [partner]:
            to_latent(src, dst.at[me_l], ssem, rsem, p, me_l).start()

    def collect(dst, ssem, rsem, use):
        @pl.loop(1, n_l // 2)
        def _(k):
            p = lax.rem(me_l + 2 * k, n_l)
            to_latent(dst.at[p], dst.at[p], ssem, rsem, p, p).wait_recv()
            pltpu.make_async_remote_copy(
                src_ref=dst.at[p], dst_ref=dst.at[p], send_sem=ssem.at[n_l + p], recv_sem=rsem.at[p],
                device_id=(me_e, partner), device_id_type=MESH).start()
            use(p)

        @pl.loop(0, n_l // 2)
        def _(k):
            p = lax.rem(partner + 2 * k, n_l)
            to_latent(dst.at[p], dst.at[p], ssem, rsem, p, p).wait_recv()
            use(p)

    def drain(src, dst, ssem, rsem):
        for p in alike + [partner]:
            to_latent(src, dst.at[me_l], ssem, rsem, p, me_l).wait_send()
        for p in alike:
            pltpu.make_async_remote_copy(
                src_ref=dst.at[p], dst_ref=dst.at[p], send_sem=ssem.at[n_l + p], recv_sem=rsem.at[p],
                device_id=(me_e, partner), device_id_type=MESH).wait_send()

    w_copy = pltpu.make_async_copy(w_hbm.at[0], w_ref, w_sem)
    w_copy.start()
    barrier = pltpu.get_barrier_semaphore()
    for p in peers(me_e, n_e):
        pl.semaphore_signal(barrier, inc=1, device_id=(p, me_l), device_id_type=MESH)
    for p in peers(me_l, n_l):
        pl.semaphore_signal(barrier, inc=1, device_id=(me_e, p), device_id_type=MESH)

    aug[...] = jnp.zeros_like(aug)
    aug[:, :width] = tok_ref[...].astype(jnp.float32)
    aug[:, width:width + list_len] = (blocks_ref[...] + 1).astype(jnp.float32)
    route = jnp.broadcast_to(route_ref[...], (8, n_tok))
    one_hot = (route == lax.broadcasted_iota(jnp.int32, (8, n_tok), 0)).astype(jnp.float32)
    before = (lax.broadcasted_iota(jnp.int32, (n_tok, n_tok), 0)
              < lax.broadcasted_iota(jnp.int32, (n_tok, n_tok), 1)).astype(jnp.float32)
    earlier = jnp.sum(jnp.dot(one_hot, before, preferred_element_type=jnp.float32) * one_hot, axis=0, keepdims=True)
    target = (route.astype(jnp.float32) * CAP + earlier).astype(jnp.bfloat16)
    repeat = (lax.broadcasted_iota(jnp.int32, (n_tok, PARTS * n_tok), 0)
              == (lax.broadcasted_iota(jnp.int32, (n_tok, PARTS * n_tok), 1) & (n_tok - 1))).astype(jnp.bfloat16)
    target = jnp.dot(target, repeat, preferred_element_type=jnp.float32)[:1]
    stacked = jnp.concatenate([aug[:, c * chunk:(c + 1) * chunk] for c in range(PARTS)], axis=0).astype(jnp.bfloat16)
    shape = (n_e * PACK, PARTS * n_tok)
    row = lax.broadcasted_iota(jnp.int32, shape, 0)
    col = lax.broadcasted_iota(jnp.int32, shape, 1)
    place = (row >> 4) * CAP + (row & 1)
    hit = (target == place.astype(jnp.float32)) & (col // n_tok == ((row >> 1) & (PARTS - 1)))
    packed = jnp.dot(hit.astype(jnp.bfloat16), stacked, preferred_element_type=jnp.float32)
    pack[...] = packed.astype(jnp.bfloat16).reshape(pack.shape)

    pl.semaphore_wait(barrier, (n_e - 1) + (n_l - 1))
    for p in peers(me_e, n_e):
        to_expert(pack.at[p], mine.at[me_e], s1, r1, p, me_e).start()
    mine[me_e] = pack[me_e]
    for p in peers(me_e, n_e):
        to_expert(pack.at[p], mine.at[p], s1, r1, p, p).wait_recv()
    shape = (n_e * PACK, n_e * PACK)
    row = lax.broadcasted_iota(jnp.int32, shape, 0)
    col = lax.broadcasted_iota(jnp.int32, shape, 1)
    unpack = (row == ((col >> 1) & (PARTS - 1)) * share + (col >> 4) * CAP + (col & 1)).astype(jnp.bfloat16)
    flat = jnp.dot(unpack, mine[...].reshape(n_e * PACK, chunk), preferred_element_type=jnp.float32)
    flat = jnp.concatenate([flat[c * share:(c + 1) * share] for c in range(PARTS)], axis=1)
    fold = gathered.shape[2]
    gathered[me_l] = jnp.concatenate([flat[:, :fold], flat[:, fold:2 * fold]], axis=0).astype(jnp.bfloat16)
    spread(gathered.at[me_l], gathered, s2, r2)

    def place_rows(source):
        block = gathered[source].astype(jnp.float32)
        at = pl.ds(pl.multiple_of(source * share, 8), share)
        rows[at, :fold] = block[:share]
        rows[at, fold:] = block[share:]

    place_rows(me_l)
    collect(gathered, s2, r2, place_rows)

    decb = decb_ref[...].reshape(1, width)
    bf = (rows[:, :width] - decb).astype(jnp.bfloat16)
    shifted[...] = bf
    left_ref[:count, :] = bf
    lists = rows[:, width:width + LANES]
    first_block = me_l * (latents // BLK)
    for b in range(latents // BLK):
        number = (first_block + b + 1).astype(jnp.float32)
        found = jnp.max((lists == number).astype(jnp.float32), axis=1, keepdims=True)
        gate[:, b * BLK:(b + 1) * BLK] = jnp.broadcast_to(found, (count, BLK))

    w_copy.wait()

    @pl.loop(0, latents // wide)
    def _(j):
        at = pl.ds(pl.multiple_of(j * wide, wide), wide)
        pre = jnp.dot(shifted[...], w_ref[:, at], preferred_element_type=jnp.float32) + encb_ref[:, at]
        mask = gate[:, at]
        right_ref[count:, at] = (jnp.maximum(pre, 0.0) * mask).astype(jnp.bfloat16)
        gate[:, at] = jnp.where(pre > 0.0, mask, 0.0)

    def folded(value):
        return jnp.concatenate([value[:, :quarter], value[:, quarter:]], axis=0)

    def unfolded(value):
        return jnp.concatenate([value[:share], value[share:]], axis=1)

    own = pl.ds(pl.multiple_of(me_l * share, 8), share)
    for h in range(2):
        @pl.loop(0, half // deep)
        def _(j):
            at = pl.ds(pl.multiple_of(h * half + j * deep, deep), deep)
            part[:, at] = lax.dot_general(
                right_ref[count:, :], w_ref[at, :], ALONG_LAST, preferred_element_type=jnp.float32)

        cols = slice(h * half, (h + 1) * half)

        @pl.loop(1, n_l)
        def _(k):
            p = lax.rem(me_l + k, n_l)
            rs_send[h, p] = folded(part[pl.ds(pl.multiple_of(p * share, 8), share), cols]).astype(jnp.bfloat16)
            to_latent(rs_send.at[h, p], rs_recv.at[h, me_l], s3.at[h], r3.at[h], p, me_l).start()

    valid = (rows[own, width:width + 1] > 0.5).astype(jnp.float32)
    loss = jnp.zeros((), jnp.float32)
    error_sum = []
    for h in range(2):
        cols = slice(h * half, (h + 1) * half)
        total = part[own, cols]
        for p in peers(me_l, n_l):
            to_latent(rs_send.at[h, p], rs_recv.at[h, p], s3.at[h], r3.at[h], p, p).wait_recv()
            total = total + unfolded(rs_recv[h, p].astype(jnp.float32))
        error = (total + decb[:, cols] - rows[own, cols]) * valid
        ag_recv[h, me_l] = folded(error).astype(jnp.bfloat16)
        spread(ag_recv.at[h, me_l], ag_recv.at[h], s4.at[h], r4.at[h])
        error_sum.append(jnp.sum(error, axis=0, keepdims=True))
        loss = loss + 0.5 * jnp.sum(error * error)
    error_sum = jnp.concatenate(error_sum, axis=1)

    for h in range(2):
        cols = slice(h * half, (h + 1) * half)

        def place_error(s):
            at = pl.ds(pl.multiple_of(s * share, 8), share)
            err[at, :] = unfolded(ag_recv[h, s].astype(jnp.float32))

        place_error(me_l)
        collect(ag_recv.at[h], s4.at[h], r4.at[h], place_error)
        left_ref[count:, cols] = err[...].astype(jnp.bfloat16)

        @pl.loop(0, latents // wide)
        def _(j):
            at = pl.ds(pl.multiple_of(j * wide, wide), wide)
            grad = jnp.dot(left_ref[count:, cols], w_ref[cols, at], preferred_element_type=jnp.float32)
            if h == 0:
                acc[:, at] = grad
            else:
                grad = (acc[:, at] + grad) * gate[:, at]
                right_ref[:count, at] = grad.astype(jnp.bfloat16)
                genc_ref[:, at] = jnp.sum(grad, axis=0, keepdims=True)

    column = jnp.broadcast_to(genc_ref[...], (8, latents)).astype(jnp.bfloat16)
    for j in range(width // TILE):
        at = slice(j * TILE, (j + 1) * TILE)
        pulled = lax.dot_general(column, w_ref[at, :], ALONG_LAST, preferred_element_type=jnp.float32)
        vec_e[me_e, :, at] = error_sum[:, at] - pulled[:1]
    vec_e[me_e, :, width:] = jnp.broadcast_to(loss.reshape(1, 1), (1, LANES))

    for p in peers(me_e, n_e):
        to_expert(vec_e.at[me_e], vec_e.at[me_e], s5, r5, p, me_e).start()
    for p in peers(me_e, n_e):
        to_expert(vec_e.at[p], vec_e.at[p], s5, r5, p, p).wait_recv()
    vec = vec_e[0]
    for s in range(1, n_e):
        vec = vec + vec_e[s]
    vec_l[me_l] = vec
    for p in peers(me_l, n_l):
        to_latent(vec_l.at[me_l], vec_l.at[me_l], s6, r6, p, me_l).start()
    for p in peers(me_l, n_l):
        to_latent(vec_l.at[p], vec_l.at[p], s6, r6, p, p).wait_recv()
    vec = vec_l[0]
    for s in range(1, n_l):
        vec = vec + vec_l[s]
    gdec_ref[...] = vec[:, :width].reshape(width)
    loss_ref[0] = vec[0, width] * (1.0 / (n_tok * n_e * n_l))

    for p in peers(me_e, n_e):
        to_expert(pack.at[p], mine.at[me_e], s1, r1, p, me_e).wait_send()
        to_expert(vec_e.at[me_e], vec_e.at[me_e], s5, r5, p, me_e).wait_send()
    for p in peers(me_l, n_l):
        to_latent(vec_l.at[me_l], vec_l.at[me_l], s6, r6, p, me_l).wait_send()
    drain(gathered.at[me_l], gathered, s2, r2)
    for h in range(2):
        drain(ag_recv.at[h, me_l], ag_recv.at[h], s4.at[h], r4.at[h])
        for p in peers(me_l, n_l):
            to_latent(rs_send.at[h, p], rs_recv.at[h, me_l], s3.at[h], r3.at[h], p, me_l).wait_send()


def grad_kernel(left_ref, right_ref, genc_in, gdec_in, loss_in, out_ref, genc_out, gdec_out, loss_out):
    @pl.when(pl.program_id(0) == 0)
    def _():
        genc_out[...] = genc_in[...]
        gdec_out[...] = gdec_in[...]
        loss_out[0] = loss_in[0]

    for j in range(right_ref.shape[1] // TILE):
        at = slice(j * TILE, (j + 1) * TILE)
        out_ref[0, :, at] = lax.dot_general(
            left_ref[...], right_ref[:, at], ALONG_FIRST, preferred_element_type=jnp.float32).astype(out_ref.dtype)


def shards(tokens, route, blocks, weight, enc_bias, dec_bias):
    n_e = lax.axis_size("expert")
    n_l = lax.axis_size("latent")
    n_tok, width = tokens.shape
    list_len = blocks.shape[1]
    latents = weight.shape[2]
    share = n_e * CAP
    count = n_l * share
    aug_width = -(-(width + LANES) // (PARTS * LANES)) * PARTS * LANES
    chunk = aug_width // PARTS
    fold = -(-(width + LANES) // (2 * LANES)) * LANES
    vmem = pl.BlockSpec(memory_space=pltpu.VMEM)
    dma = pltpu.SemaphoreType.DMA
    f32, bf16 = jnp.float32, jnp.bfloat16
    left, right, genc, gdec, loss = pl.pallas_call(
        functools.partial(step_kernel, n_e, n_l, n_tok, width, list_len),
        out_shape=(
            jax.ShapeDtypeStruct((2 * count, width), bf16),
            jax.ShapeDtypeStruct((2 * count, latents), bf16),
            jax.ShapeDtypeStruct((1, latents), f32),
            jax.ShapeDtypeStruct((width,), f32),
            jax.ShapeDtypeStruct((1,), f32),
        ),
        in_specs=[vmem, vmem, vmem, pl.BlockSpec(memory_space=pl.ANY), vmem, vmem],
        out_specs=[vmem] * 4 + [pl.BlockSpec(memory_space=pltpu.SMEM)],
        scratch_shapes=[
            pltpu.VMEM((width, latents), bf16),
            pltpu.VMEM((n_tok, aug_width), f32),
            pltpu.VMEM((n_e, PACK, chunk), bf16),
            pltpu.VMEM((n_e, PACK, chunk), bf16),
            pltpu.VMEM((n_l, 2 * share, fold), bf16),
            pltpu.VMEM((count, 2 * fold), f32),
            pltpu.VMEM((count, width), bf16),
            pltpu.VMEM((count, latents), f32),
            pltpu.VMEM((count, width), f32),
            pltpu.VMEM((2, n_l, 2 * share, width // 4), bf16),
            pltpu.VMEM((2, n_l, 2 * share, width // 4), bf16),
            pltpu.VMEM((2, n_l, 2 * share, width // 4), bf16),
            pltpu.VMEM((count, width // 2), f32),
            pltpu.VMEM((count, latents), f32),
            pltpu.VMEM((n_e, 1, width + LANES), f32),
            pltpu.VMEM((n_l, 1, width + LANES), f32),
            dma,
            dma((n_e,)), dma((n_e,)),
            dma((2 * n_l,)), dma((n_l,)),
            dma((2, n_l)), dma((2, n_l)),
            dma((2, 2 * n_l)), dma((2, n_l)),
            dma((n_e,)), dma((n_e,)),
            dma((n_l,)), dma((n_l,)),
        ],
        compiler_params=pltpu.CompilerParams(
            collective_id=0, has_side_effects=True, vmem_limit_bytes=56 << 20),
        name="sae_step",
    )(tokens, route.reshape(1, n_tok), blocks, weight, enc_bias, dec_bias)
    strip = TILE
    small = [
        pl.BlockSpec((1, latents), lambda i: (0, 0)),
        pl.BlockSpec((width,), lambda i: (0,)),
        pl.BlockSpec(memory_space=pltpu.SMEM),
    ]
    grad, genc, gdec, loss = pl.pallas_call(
        grad_kernel,
        out_shape=(
            jax.ShapeDtypeStruct((1, width, latents), bf16),
            jax.ShapeDtypeStruct((1, latents), f32),
            jax.ShapeDtypeStruct((width,), f32),
            jax.ShapeDtypeStruct((1,), f32),
        ),
        grid=(width // strip,),
        in_specs=[
            pl.BlockSpec((2 * count, strip), lambda i: (0, i)),
            pl.BlockSpec((2 * count, latents), lambda i: (0, 0)),
        ] + small,
        out_specs=[pl.BlockSpec((1, strip, latents), lambda i: (0, i, 0))] + small,
        compiler_params=pltpu.CompilerParams(vmem_limit_bytes=56 << 20),
        name="grad_weight",
    )(left, right, genc, gdec, loss)
    return grad, genc, gdec, loss[0]


def solution(mesh):
    return jax.shard_map(
        shards,
        mesh=mesh,
        in_specs=(
            P(("expert", "latent"), None),
            P(("expert", "latent"), None),
            P(("expert", "latent"), None),
            P("expert", None, "latent"),
            P("expert", "latent"),
            P(),
        ),
        out_specs=(P("expert", None, "latent"), P("expert", "latent"), P(), P()),
        check_vma=False,
    )
```

```python
import functools
import jax
import jax.numpy as jnp
from jax import lax
from jax.experimental import pallas as pl
from jax.experimental.pallas import tpu as pltpu
from jax.sharding import PartitionSpec as P

BLK = 128
CAP = 2
PACK = 16
PARTS = PACK // CAP
LANES = 128
TILE = 256
MESH = pl.DeviceIdType.MESH
ALONG_LAST = (((1,), (1,)), ((), ()))
ALONG_FIRST = (((0,), (0,)), ((), ()))


def step_kernel(
    n_e, n_l, n_tok, width, list_len,
    tok_ref, route_ref, blocks_ref, w_hbm, encb_ref, decb_ref,
    left_ref, right_ref, genc_ref, gdec_ref, loss_ref,
    w_ref, aug, pack, mine, gathered, rows, shifted, gate, part, rs_send, rs_recv, ag_recv, err, acc, vec_e, vec_l,
    w_sem, s1, r1, s2, r2, s3, r3, s4, r4, s5, r5, s6, r6,
):
    me_e = lax.axis_index("expert")
    me_l = lax.axis_index("latent")
    share = n_e * CAP
    count = n_l * share
    half = width // 2
    quarter = half // 2
    chunk = aug.shape[1] // PARTS
    latents = w_ref.shape[1]
    few = count <= LANES
    wide = latents if few else TILE
    deep = half if few else TILE

    def to_expert(src, dst, ssem, rsem, peer, slot):
        return pltpu.make_async_remote_copy(
            src_ref=src, dst_ref=dst, send_sem=ssem.at[peer], recv_sem=rsem.at[slot],
            device_id=(peer, me_l), device_id_type=MESH)

    def to_latent(src, dst, ssem, rsem, peer, slot):
        return pltpu.make_async_remote_copy(
            src_ref=src, dst_ref=dst, send_sem=ssem.at[peer], recv_sem=rsem.at[slot],
            device_id=(me_e, peer), device_id_type=MESH)

    def peers(me, n):
        return [lax.rem(me + k, n) for k in range(1, n)]

    partner = me_l + 1 - 2 * lax.rem(me_l, 2)
    alike = [lax.rem(me_l + 2 * k, n_l) for k in range(1, n_l // 2)]

    def spread(src, dst, ssem, rsem):
        for p in alike + [partner]:
            to_latent(src, dst.at[me_l], ssem, rsem, p, me_l).start()

    def collect(dst, ssem, rsem, use):
        @pl.loop(1, n_l // 2)
        def _(k):
            p = lax.rem(me_l + 2 * k, n_l)
            to_latent(dst.at[p], dst.at[p], ssem, rsem, p, p).wait_recv()
            pltpu.make_async_remote_copy(
                src_ref=dst.at[p], dst_ref=dst.at[p], send_sem=ssem.at[n_l + p], recv_sem=rsem.at[p],
                device_id=(me_e, partner), device_id_type=MESH).start()
            use(p)

        @pl.loop(0, n_l // 2)
        def _(k):
            p = lax.rem(partner + 2 * k, n_l)
            to_latent(dst.at[p], dst.at[p], ssem, rsem, p, p).wait_recv()
            use(p)

    def drain(src, dst, ssem, rsem):
        for p in alike + [partner]:
            to_latent(src, dst.at[me_l], ssem, rsem, p, me_l).wait_send()
        for p in alike:
            pltpu.make_async_remote_copy(
                src_ref=dst.at[p], dst_ref=dst.at[p], send_sem=ssem.at[n_l + p], recv_sem=rsem.at[p],
                device_id=(me_e, partner), device_id_type=MESH).wait_send()

    w_copy = pltpu.make_async_copy(w_hbm.at[0], w_ref, w_sem)
    w_copy.start()
    barrier = pltpu.get_barrier_semaphore()
    for p in peers(me_e, n_e):
        pl.semaphore_signal(barrier, inc=1, device_id=(p, me_l), device_id_type=MESH)
    for p in peers(me_l, n_l):
        pl.semaphore_signal(barrier, inc=1, device_id=(me_e, p), device_id_type=MESH)

    aug[...] = jnp.zeros_like(aug)
    aug[:, :width] = tok_ref[...].astype(jnp.float32)
    aug[:, width:width + list_len] = (blocks_ref[...] + 1).astype(jnp.float32)
    route = jnp.broadcast_to(route_ref[...], (8, n_tok))
    one_hot = (route == lax.broadcasted_iota(jnp.int32, (8, n_tok), 0)).astype(jnp.float32)
    before = (lax.broadcasted_iota(jnp.int32, (n_tok, n_tok), 0)
              < lax.broadcasted_iota(jnp.int32, (n_tok, n_tok), 1)).astype(jnp.float32)
    earlier = jnp.sum(jnp.dot(one_hot, before, preferred_element_type=jnp.float32) * one_hot, axis=0, keepdims=True)
    target = (route.astype(jnp.float32) * CAP + earlier).astype(jnp.bfloat16)
    repeat = (lax.broadcasted_iota(jnp.int32, (n_tok, PARTS * n_tok), 0)
              == (lax.broadcasted_iota(jnp.int32, (n_tok, PARTS * n_tok), 1) & (n_tok - 1))).astype(jnp.bfloat16)
    target = jnp.dot(target, repeat, preferred_element_type=jnp.float32)[:1]
    stacked = jnp.concatenate([aug[:, c * chunk:(c + 1) * chunk] for c in range(PARTS)], axis=0).astype(jnp.bfloat16)
    shape = (n_e * PACK, PARTS * n_tok)
    row = lax.broadcasted_iota(jnp.int32, shape, 0)
    col = lax.broadcasted_iota(jnp.int32, shape, 1)
    place = (row >> 4) * CAP + (row & 1)
    hit = (target == place.astype(jnp.float32)) & (col // n_tok == ((row >> 1) & (PARTS - 1)))
    packed = jnp.dot(hit.astype(jnp.bfloat16), stacked, preferred_element_type=jnp.float32)
    pack[...] = packed.astype(jnp.bfloat16).reshape(pack.shape)

    pl.semaphore_wait(barrier, (n_e - 1) + (n_l - 1))
    for p in peers(me_e, n_e):
        to_expert(pack.at[p], mine.at[me_e], s1, r1, p, me_e).start()
    mine[me_e] = pack[me_e]
    for p in peers(me_e, n_e):
        to_expert(pack.at[p], mine.at[p], s1, r1, p, p).wait_recv()
    shape = (n_e * PACK, n_e * PACK)
    row = lax.broadcasted_iota(jnp.int32, shape, 0)
    col = lax.broadcasted_iota(jnp.int32, shape, 1)
    unpack = (row == ((col >> 1) & (PARTS - 1)) * share + (col >> 4) * CAP + (col & 1)).astype(jnp.bfloat16)
    flat = jnp.dot(unpack, mine[...].reshape(n_e * PACK, chunk), preferred_element_type=jnp.float32)
    flat = jnp.concatenate([flat[c * share:(c + 1) * share] for c in range(PARTS)], axis=1)
    fold = gathered.shape[2]
    gathered[me_l] = jnp.concatenate([flat[:, :fold], flat[:, fold:2 * fold]], axis=0).astype(jnp.bfloat16)
    spread(gathered.at[me_l], gathered, s2, r2)

    def place_rows(source):
        block = gathered[source].astype(jnp.float32)
        at = pl.ds(pl.multiple_of(source * share, 8), share)
        rows[at, :fold] = block[:share]
        rows[at, fold:] = block[share:]

    place_rows(me_l)
    collect(gathered, s2, r2, place_rows)

    decb = decb_ref[...].reshape(1, width)
    bf = (rows[:, :width] - decb).astype(jnp.bfloat16)
    shifted[...] = bf
    left_ref[:count, :] = bf
    lists = rows[:, width:width + LANES]
    first_block = me_l * (latents // BLK)
    for b in range(latents // BLK):
        number = (first_block + b + 1).astype(jnp.float32)
        found = jnp.max((lists == number).astype(jnp.float32), axis=1, keepdims=True)
        gate[:, b * BLK:(b + 1) * BLK] = jnp.broadcast_to(found, (count, BLK))

    w_copy.wait()

    @pl.loop(0, latents // wide)
    def _(j):
        at = pl.ds(pl.multiple_of(j * wide, wide), wide)
        pre = jnp.dot(shifted[...], w_ref[:, at], preferred_element_type=jnp.float32) + encb_ref[:, at]
        mask = gate[:, at]
        right_ref[count:, at] = (jnp.maximum(pre, 0.0) * mask).astype(jnp.bfloat16)
        gate[:, at] = jnp.where(pre > 0.0, mask, 0.0)

    def folded(value):
        return jnp.concatenate([value[:, :quarter], value[:, quarter:]], axis=0)

    def unfolded(value):
        return jnp.concatenate([value[:share], value[share:]], axis=1)

    own = pl.ds(pl.multiple_of(me_l * share, 8), share)
    for h in range(2):
        @pl.loop(0, half // deep)
        def _(j):
            at = pl.ds(pl.multiple_of(h * half + j * deep, deep), deep)
            part[:, at] = lax.dot_general(
                right_ref[count:, :], w_ref[at, :], ALONG_LAST, preferred_element_type=jnp.float32)

        cols = slice(h * half, (h + 1) * half)

        @pl.loop(1, n_l)
        def _(k):
            p = lax.rem(me_l + k, n_l)
            rs_send[h, p] = folded(part[pl.ds(pl.multiple_of(p * share, 8), share), cols]).astype(jnp.bfloat16)
            to_latent(rs_send.at[h, p], rs_recv.at[h, me_l], s3.at[h], r3.at[h], p, me_l).start()

    valid = (rows[own, width:width + 1] > 0.5).astype(jnp.float32)
    loss = jnp.zeros((), jnp.float32)
    error_sum = []
    for h in range(2):
        cols = slice(h * half, (h + 1) * half)
        total = part[own, cols]
        for p in peers(me_l, n_l):
            to_latent(rs_send.at[h, p], rs_recv.at[h, p], s3.at[h], r3.at[h], p, p).wait_recv()
            total = total + unfolded(rs_recv[h, p].astype(jnp.float32))
        error = (total + decb[:, cols] - rows[own, cols]) * valid
        ag_recv[h, me_l] = folded(error).astype(jnp.bfloat16)
        for p in peers(me_l, n_l):
            to_latent(ag_recv.at[h, me_l], ag_recv.at[h, me_l], s4.at[h], r4.at[h], p, me_l).start()
        error_sum.append(jnp.sum(error, axis=0, keepdims=True))
        loss = loss + 0.5 * jnp.sum(error * error)
    error_sum = jnp.concatenate(error_sum, axis=1)

    for h in range(2):
        cols = slice(h * half, (h + 1) * half)

        def place_error(s):
            at = pl.ds(pl.multiple_of(s * share, 8), share)
            err[at, :] = unfolded(ag_recv[h, s].astype(jnp.float32))

        place_error(me_l)

        @pl.loop(1, n_l)
        def _(k):
            p = lax.rem(me_l + k, n_l)
            to_latent(ag_recv.at[h, p], ag_recv.at[h, p], s4.at[h], r4.at[h], p, p).wait_recv()
            place_error(p)

        left_ref[count:, cols] = err[...].astype(jnp.bfloat16)

        @pl.loop(0, latents // wide)
        def _(j):
            at = pl.ds(pl.multiple_of(j * wide, wide), wide)
            grad = jnp.dot(left_ref[count:, cols], w_ref[cols, at], preferred_element_type=jnp.float32)
            if h == 0:
                acc[:, at] = grad
            else:
                grad = (acc[:, at] + grad) * gate[:, at]
                right_ref[:count, at] = grad.astype(jnp.bfloat16)
                genc_ref[:, at] = jnp.sum(grad, axis=0, keepdims=True)

    column = jnp.broadcast_to(genc_ref[...], (8, latents)).astype(jnp.bfloat16)
    for j in range(width // TILE):
        at = slice(j * TILE, (j + 1) * TILE)
        pulled = lax.dot_general(column, w_ref[at, :], ALONG_LAST, preferred_element_type=jnp.float32)
        vec_e[me_e, :, at] = error_sum[:, at] - pulled[:1]
    vec_e[me_e, :, width:] = jnp.broadcast_to(loss.reshape(1, 1), (1, LANES))

    for p in peers(me_e, n_e):
        to_expert(vec_e.at[me_e], vec_e.at[me_e], s5, r5, p, me_e).start()
    for p in peers(me_e, n_e):
        to_expert(vec_e.at[p], vec_e.at[p], s5, r5, p, p).wait_recv()
    vec = vec_e[0]
    for s in range(1, n_e):
        vec = vec + vec_e[s]
    vec_l[me_l] = vec
    for p in peers(me_l, n_l):
        to_latent(vec_l.at[me_l], vec_l.at[me_l], s6, r6, p, me_l).start()
    for p in peers(me_l, n_l):
        to_latent(vec_l.at[p], vec_l.at[p], s6, r6, p, p).wait_recv()
    vec = vec_l[0]
    for s in range(1, n_l):
        vec = vec + vec_l[s]
    gdec_ref[...] = vec[:, :width].reshape(width)
    loss_ref[0] = vec[0, width] * (1.0 / (n_tok * n_e * n_l))

    for p in peers(me_e, n_e):
        to_expert(pack.at[p], mine.at[me_e], s1, r1, p, me_e).wait_send()
        to_expert(vec_e.at[me_e], vec_e.at[me_e], s5, r5, p, me_e).wait_send()
    for p in peers(me_l, n_l):
        to_latent(vec_l.at[me_l], vec_l.at[me_l], s6, r6, p, me_l).wait_send()
    drain(gathered.at[me_l], gathered, s2, r2)
    for h in range(2):
        for p in peers(me_l, n_l):
            to_latent(rs_send.at[h, p], rs_recv.at[h, me_l], s3.at[h], r3.at[h], p, me_l).wait_send()
            to_latent(ag_recv.at[h, me_l], ag_recv.at[h, me_l], s4.at[h], r4.at[h], p, me_l).wait_send()


def grad_kernel(left_ref, right_ref, genc_in, gdec_in, loss_in, out_ref, genc_out, gdec_out, loss_out, grad, sems):
    width = grad.shape[0]
    strip = width // sems.shape[0]
    copies = []
    for i in range(sems.shape[0]):
        at = slice(i * strip, (i + 1) * strip)
        grad[at, :] = lax.dot_general(
            left_ref[:, at], right_ref[...], ALONG_FIRST, preferred_element_type=jnp.float32).astype(grad.dtype)
        copies.append(pltpu.make_async_copy(grad.at[at, :], out_ref.at[0, at, :], sems.at[i]))
        copies[-1].start()
    genc_out[...] = genc_in[...]
    gdec_out[...] = gdec_in[...]
    loss_out[0] = loss_in[0]
    for copy in copies:
        copy.wait()


def shards(tokens, route, blocks, weight, enc_bias, dec_bias):
    n_e = lax.axis_size("expert")
    n_l = lax.axis_size("latent")
    n_tok, width = tokens.shape
    list_len = blocks.shape[1]
    latents = weight.shape[2]
    share = n_e * CAP
    count = n_l * share
    aug_width = -(-(width + LANES) // (PARTS * LANES)) * PARTS * LANES
    chunk = aug_width // PARTS
    fold = -(-(width + LANES) // (2 * LANES)) * LANES
    vmem = pl.BlockSpec(memory_space=pltpu.VMEM)
    dma = pltpu.SemaphoreType.DMA
    f32, bf16 = jnp.float32, jnp.bfloat16
    left, right, genc, gdec, loss = pl.pallas_call(
        functools.partial(step_kernel, n_e, n_l, n_tok, width, list_len),
        out_shape=(
            jax.ShapeDtypeStruct((2 * count, width), bf16),
            jax.ShapeDtypeStruct((2 * count, latents), bf16),
            jax.ShapeDtypeStruct((1, latents), f32),
            jax.ShapeDtypeStruct((width,), f32),
            jax.ShapeDtypeStruct((1,), f32),
        ),
        in_specs=[vmem, vmem, vmem, pl.BlockSpec(memory_space=pl.ANY), vmem, vmem],
        out_specs=[vmem] * 4 + [pl.BlockSpec(memory_space=pltpu.SMEM)],
        scratch_shapes=[
            pltpu.VMEM((width, latents), bf16),
            pltpu.VMEM((n_tok, aug_width), f32),
            pltpu.VMEM((n_e, PACK, chunk), bf16),
            pltpu.VMEM((n_e, PACK, chunk), bf16),
            pltpu.VMEM((n_l, 2 * share, fold), bf16),
            pltpu.VMEM((count, 2 * fold), f32),
            pltpu.VMEM((count, width), bf16),
            pltpu.VMEM((count, latents), f32),
            pltpu.VMEM((count, width), f32),
            pltpu.VMEM((2, n_l, 2 * share, width // 4), bf16),
            pltpu.VMEM((2, n_l, 2 * share, width // 4), bf16),
            pltpu.VMEM((2, n_l, 2 * share, width // 4), bf16),
            pltpu.VMEM((count, width // 2), f32),
            pltpu.VMEM((count, latents), f32),
            pltpu.VMEM((n_e, 1, width + LANES), f32),
            pltpu.VMEM((n_l, 1, width + LANES), f32),
            dma,
            dma((n_e,)), dma((n_e,)),
            dma((2 * n_l,)), dma((n_l,)),
            dma((2, n_l)), dma((2, n_l)),
            dma((2, n_l)), dma((2, n_l)),
            dma((n_e,)), dma((n_e,)),
            dma((n_l,)), dma((n_l,)),
        ],
        compiler_params=pltpu.CompilerParams(
            collective_id=0, has_side_effects=True, vmem_limit_bytes=56 << 20),
        name="sae_step",
    )(tokens, route.reshape(1, n_tok), blocks, weight, enc_bias, dec_bias)
    small = [vmem, vmem, pl.BlockSpec(memory_space=pltpu.SMEM)]
    grad, genc, gdec, loss = pl.pallas_call(
        grad_kernel,
        out_shape=(
            jax.ShapeDtypeStruct((1, width, latents), bf16),
            jax.ShapeDtypeStruct((1, latents), f32),
            jax.ShapeDtypeStruct((width,), f32),
            jax.ShapeDtypeStruct((1,), f32),
        ),
        in_specs=[vmem, vmem] + small,
        out_specs=[pl.BlockSpec(memory_space=pl.ANY)] + small,
        scratch_shapes=[pltpu.VMEM((width, latents), bf16), dma((width // TILE,))],
        compiler_params=pltpu.CompilerParams(vmem_limit_bytes=56 << 20),
        name="grad_weight",
    )(left, right, genc, gdec, loss)
    return grad, genc, gdec, loss[0]


def solution(mesh):
    return jax.shard_map(
        shards,
        mesh=mesh,
        in_specs=(
            P(("expert", "latent"), None),
            P(("expert", "latent"), None),
            P(("expert", "latent"), None),
            P("expert", None, "latent"),
            P("expert", "latent"),
            P(),
        ),
        out_specs=(P("expert", None, "latent"), P("expert", "latent"), P(), P()),
        check_vma=False,
    )
```

```python
import functools
import jax
import jax.numpy as jnp
from jax import lax
from jax.experimental import pallas as pl
from jax.experimental.pallas import tpu as pltpu
from jax.sharding import PartitionSpec as P

BLK = 128
CAP = 2
PACK = 16
PARTS = PACK // CAP
LANES = 128
TILE = 256
MESH = pl.DeviceIdType.MESH
ALONG_LAST = (((1,), (1,)), ((), ()))
ALONG_FIRST = (((0,), (0,)), ((), ()))


def step_kernel(
    n_e, n_l, n_tok, width, list_len,
    tok_ref, route_ref, blocks_ref, w_hbm, encb_ref, decb_ref,
    left_out, right_out, genc_ref, gdec_ref, loss_ref,
    left_ref, right_ref, w_ref, aug, pack, mine, gathered, rows, shifted, gate, part, rs_send, rs_recv, ag_recv, err, acc, vec_e, vec_l,
    w_sem, out_sem, s1, r1, s2, r2, s3, r3, s4, r4, s5, r5, s6, r6,
):
    me_e = lax.axis_index("expert")
    me_l = lax.axis_index("latent")
    share = n_e * CAP
    count = n_l * share
    half = width // 2
    quarter = half // 2
    chunk = aug.shape[1] // PARTS
    latents = w_ref.shape[1]
    few = count <= LANES
    wide = latents if few else TILE
    deep = half if few else TILE

    def to_expert(src, dst, ssem, rsem, peer, slot):
        return pltpu.make_async_remote_copy(
            src_ref=src, dst_ref=dst, send_sem=ssem.at[peer], recv_sem=rsem.at[slot],
            device_id=(peer, me_l), device_id_type=MESH)

    def to_latent(src, dst, ssem, rsem, peer, slot):
        return pltpu.make_async_remote_copy(
            src_ref=src, dst_ref=dst, send_sem=ssem.at[peer], recv_sem=rsem.at[slot],
            device_id=(me_e, peer), device_id_type=MESH)

    def steps(n):
        if n == 1:
            return lambda body: body(0)
        return pl.loop(0, n)

    def peers(me, n):
        return [lax.rem(me + k, n) for k in range(1, n)]

    partner = me_l + 1 - 2 * lax.rem(me_l, 2)
    alike = [lax.rem(me_l + 2 * k, n_l) for k in range(1, n_l // 2)]

    def spread(src, dst, ssem, rsem):
        for p in alike + [partner]:
            to_latent(src, dst.at[me_l], ssem, rsem, p, me_l).start()

    def collect(dst, ssem, rsem, use):
        @pl.loop(1, n_l // 2)
        def _(k):
            p = lax.rem(me_l + 2 * k, n_l)
            to_latent(dst.at[p], dst.at[p], ssem, rsem, p, p).wait_recv()
            pltpu.make_async_remote_copy(
                src_ref=dst.at[p], dst_ref=dst.at[p], send_sem=ssem.at[n_l + p], recv_sem=rsem.at[p],
                device_id=(me_e, partner), device_id_type=MESH).start()
            use(p)

        @pl.loop(0, n_l // 2)
        def _(k):
            p = lax.rem(partner + 2 * k, n_l)
            to_latent(dst.at[p], dst.at[p], ssem, rsem, p, p).wait_recv()
            use(p)

    def drain(src, dst, ssem, rsem):
        for p in alike + [partner]:
            to_latent(src, dst.at[me_l], ssem, rsem, p, me_l).wait_send()
        for p in alike:
            pltpu.make_async_remote_copy(
                src_ref=dst.at[p], dst_ref=dst.at[p], send_sem=ssem.at[n_l + p], recv_sem=rsem.at[p],
                device_id=(me_e, partner), device_id_type=MESH).wait_send()

    barrier = pltpu.get_barrier_semaphore()
    for p in peers(me_e, n_e):
        pl.semaphore_signal(barrier, inc=1, device_id=(p, me_l), device_id_type=MESH)
    for p in peers(me_l, n_l):
        pl.semaphore_signal(barrier, inc=1, device_id=(me_e, p), device_id_type=MESH)

    w_copy = pltpu.make_async_copy(w_hbm.at[0], w_ref, w_sem)
    w_copy.start()

    aug[...] = jnp.zeros_like(aug)
    aug[:, :width] = tok_ref[...].astype(jnp.float32)
    aug[:, width:width + list_len] = (blocks_ref[...] + 1).astype(jnp.float32)
    route = jnp.broadcast_to(route_ref[...], (8, n_tok))
    one_hot = (route == lax.broadcasted_iota(jnp.int32, (8, n_tok), 0)).astype(jnp.float32)
    before = (lax.broadcasted_iota(jnp.int32, (n_tok, n_tok), 0)
              < lax.broadcasted_iota(jnp.int32, (n_tok, n_tok), 1)).astype(jnp.float32)
    earlier = jnp.sum(jnp.dot(one_hot, before, preferred_element_type=jnp.float32) * one_hot, axis=0, keepdims=True)
    target = (route.astype(jnp.float32) * CAP + earlier).astype(jnp.bfloat16)
    repeat = (lax.broadcasted_iota(jnp.int32, (n_tok, PARTS * n_tok), 0)
              == (lax.broadcasted_iota(jnp.int32, (n_tok, PARTS * n_tok), 1) & (n_tok - 1))).astype(jnp.bfloat16)
    target = jnp.dot(target, repeat, preferred_element_type=jnp.float32)[:1]
    stacked = jnp.concatenate([aug[:, c * chunk:(c + 1) * chunk] for c in range(PARTS)], axis=0).astype(jnp.bfloat16)
    shape = (n_e * PACK, PARTS * n_tok)
    row = lax.broadcasted_iota(jnp.int32, shape, 0)
    col = lax.broadcasted_iota(jnp.int32, shape, 1)
    place = (row >> 4) * CAP + (row & 1)
    hit = (target == place.astype(jnp.float32)) & (col // n_tok == ((row >> 1) & (PARTS - 1)))
    packed = jnp.dot(hit.astype(jnp.bfloat16), stacked, preferred_element_type=jnp.float32)
    pack[...] = packed.astype(jnp.bfloat16).reshape(pack.shape)

    pl.semaphore_wait(barrier, (n_e - 1) + (n_l - 1))
    for p in peers(me_e, n_e):
        to_expert(pack.at[p], mine.at[me_e], s1, r1, p, me_e).start()
    mine[me_e] = pack[me_e]
    for p in peers(me_e, n_e):
        to_expert(pack.at[p], mine.at[p], s1, r1, p, p).wait_recv()
    shape = (n_e * PACK, n_e * PACK)
    row = lax.broadcasted_iota(jnp.int32, shape, 0)
    col = lax.broadcasted_iota(jnp.int32, shape, 1)
    unpack = (row == ((col >> 1) & (PARTS - 1)) * share + (col >> 4) * CAP + (col & 1)).astype(jnp.bfloat16)
    flat = jnp.dot(unpack, mine[...].reshape(n_e * PACK, chunk), preferred_element_type=jnp.float32)
    flat = jnp.concatenate([flat[c * share:(c + 1) * share] for c in range(PARTS)], axis=1)
    fold = gathered.shape[2]
    gathered[me_l] = jnp.concatenate([flat[:, :fold], flat[:, fold:2 * fold]], axis=0).astype(jnp.bfloat16)
    spread(gathered.at[me_l], gathered, s2, r2)

    def place_rows(source):
        block = gathered[source].astype(jnp.float32)
        at = pl.ds(pl.multiple_of(source * share, 8), share)
        rows[at, :fold] = block[:share]
        rows[at, fold:] = block[share:]

    place_rows(me_l)
    collect(gathered, s2, r2, place_rows)

    decb = decb_ref[...].reshape(1, width)
    bf = (rows[:, :width] - decb).astype(jnp.bfloat16)
    shifted[...] = bf
    left_ref[:count, :] = bf
    lists = rows[:, width:width + LANES]
    first_block = me_l * (latents // BLK)
    for b in range(latents // BLK):
        number = (first_block + b + 1).astype(jnp.float32)
        found = jnp.max((lists == number).astype(jnp.float32), axis=1, keepdims=True)
        gate[:, b * BLK:(b + 1) * BLK] = jnp.broadcast_to(found, (count, BLK))

    w_copy.wait()

    @steps(latents // wide)
    def _(j):
        at = pl.ds(j * wide if few else pl.multiple_of(j * wide, wide), wide)
        pre = jnp.dot(shifted[...], w_ref[:, at], preferred_element_type=jnp.float32) + encb_ref[:, at]
        mask = gate[:, at]
        right_ref[count:, at] = (jnp.maximum(pre, 0.0) * mask).astype(jnp.bfloat16)
        gate[:, at] = jnp.where(pre > 0.0, mask, 0.0)

    def folded(value):
        return jnp.concatenate([value[:, :quarter], value[:, quarter:]], axis=0)

    def unfolded(value):
        return jnp.concatenate([value[:share], value[share:]], axis=1)

    own = pl.ds(pl.multiple_of(me_l * share, 8), share)
    for h in range(2):
        @steps(half // deep)
        def _(j):
            at = pl.ds(h * half + j * deep if few else pl.multiple_of(h * half + j * deep, deep), deep)
            part[:, at] = lax.dot_general(
                right_ref[count:, :], w_ref[at, :], ALONG_LAST, preferred_element_type=jnp.float32)

        cols = slice(h * half, (h + 1) * half)

        @pl.loop(1, n_l)
        def _(k):
            p = lax.rem(me_l + k, n_l)
            rs_send[h, p] = folded(part[pl.ds(pl.multiple_of(p * share, 8), share), cols]).astype(jnp.bfloat16)
            to_latent(rs_send.at[h, p], rs_recv.at[h, me_l], s3.at[h], r3.at[h], p, me_l).start()

    valid = (rows[own, width:width + 1] > 0.5).astype(jnp.float32)
    loss = jnp.zeros((), jnp.float32)
    error_sum = []
    for h in range(2):
        cols = slice(h * half, (h + 1) * half)
        total = part[own, cols]
        for p in peers(me_l, n_l):
            to_latent(rs_send.at[h, p], rs_recv.at[h, p], s3.at[h], r3.at[h], p, p).wait_recv()
            total = total + unfolded(rs_recv[h, p].astype(jnp.float32))
        error = (total + decb[:, cols] - rows[own, cols]) * valid
        ag_recv[h, me_l] = folded(error).astype(jnp.bfloat16)
        for p in peers(me_l, n_l):
            to_latent(ag_recv.at[h, me_l], ag_recv.at[h, me_l], s4.at[h], r4.at[h], p, me_l).start()
        error_sum.append(jnp.sum(error, axis=0, keepdims=True))
        loss = loss + 0.5 * jnp.sum(error * error)
    error_sum = jnp.concatenate(error_sum, axis=1)

    for h in range(2):
        cols = slice(h * half, (h + 1) * half)

        def place_error(s):
            at = pl.ds(pl.multiple_of(s * share, 8), share)
            err[at, :] = unfolded(ag_recv[h, s].astype(jnp.float32))

        place_error(me_l)

        @pl.loop(1, n_l)
        def _(k):
            p = lax.rem(me_l + k, n_l)
            to_latent(ag_recv.at[h, p], ag_recv.at[h, p], s4.at[h], r4.at[h], p, p).wait_recv()
            place_error(p)

        left_ref[count:, cols] = err[...].astype(jnp.bfloat16)

        @steps(latents // wide)
        def _(j):
            at = pl.ds(j * wide if few else pl.multiple_of(j * wide, wide), wide)
            grad = jnp.dot(left_ref[count:, cols], w_ref[cols, at], preferred_element_type=jnp.float32)
            if h == 0:
                acc[:, at] = grad
            else:
                grad = (acc[:, at] + grad) * gate[:, at]
                right_ref[:count, at] = grad.astype(jnp.bfloat16)
                genc_ref[:, at] = jnp.sum(grad, axis=0, keepdims=True)

    stores = [pltpu.make_async_copy(left_ref, left_out, out_sem.at[0]),
              pltpu.make_async_copy(right_ref, right_out, out_sem.at[1])]
    for copy in stores:
        copy.start()

    column = jnp.broadcast_to(genc_ref[...], (8, latents)).astype(jnp.bfloat16)
    for h in range(2):
        for j in range(half // TILE):
            at = slice(h * half + j * TILE, h * half + (j + 1) * TILE)
            pulled = lax.dot_general(column, w_ref[at, :], ALONG_LAST, preferred_element_type=jnp.float32)
            vec_e[h, me_e, :, j * TILE:(j + 1) * TILE] = error_sum[:, at] - pulled[:1]
        vec_e[h, me_e, :, half:] = jnp.broadcast_to(loss.reshape(1, 1), (1, LANES))
        for p in peers(me_e, n_e):
            to_expert(vec_e.at[h, me_e], vec_e.at[h, me_e], s5.at[h], r5.at[h], p, me_e).start()
    for h in range(2):
        for p in peers(me_e, n_e):
            to_expert(vec_e.at[h, p], vec_e.at[h, p], s5.at[h], r5.at[h], p, p).wait_recv()
        vec = vec_e[h, 0]
        for s in range(1, n_e):
            vec = vec + vec_e[h, s]
        vec_l[h, me_l] = vec
        for p in peers(me_l, n_l):
            to_latent(vec_l.at[h, me_l], vec_l.at[h, me_l], s6.at[h], r6.at[h], p, me_l).start()
    ends = []
    for h in range(2):
        for p in peers(me_l, n_l):
            to_latent(vec_l.at[h, p], vec_l.at[h, p], s6.at[h], r6.at[h], p, p).wait_recv()
        vec = vec_l[h, 0]
        for s in range(1, n_l):
            vec = vec + vec_l[h, s]
        ends.append(vec)
    gdec_ref[...] = jnp.concatenate([ends[0][:, :half], ends[1][:, :half]], axis=1).reshape(width)
    loss_ref[0] = ends[0][0, half] * (1.0 / (n_tok * n_e * n_l))
    for copy in stores:
        copy.wait()

    for p in peers(me_e, n_e):
        to_expert(pack.at[p], mine.at[me_e], s1, r1, p, me_e).wait_send()
        for h in range(2):
            to_expert(vec_e.at[h, me_e], vec_e.at[h, me_e], s5.at[h], r5.at[h], p, me_e).wait_send()
    drain(gathered.at[me_l], gathered, s2, r2)
    for h in range(2):
        for p in peers(me_l, n_l):
            to_latent(rs_send.at[h, p], rs_recv.at[h, me_l], s3.at[h], r3.at[h], p, me_l).wait_send()
            to_latent(vec_l.at[h, me_l], vec_l.at[h, me_l], s6.at[h], r6.at[h], p, me_l).wait_send()
            to_latent(ag_recv.at[h, me_l], ag_recv.at[h, me_l], s4.at[h], r4.at[h], p, me_l).wait_send()


def grad_kernel(left_ref, right_ref, genc_in, gdec_in, loss_in, out_ref, genc_out, gdec_out, loss_out, grad, sems):
    width = grad.shape[0]
    strip = width // sems.shape[0]
    copies = []
    for i in range(sems.shape[0]):
        at = slice(i * strip, (i + 1) * strip)
        grad[at, :] = lax.dot_general(
            left_ref[:, at], right_ref[...], ALONG_FIRST, preferred_element_type=jnp.float32).astype(grad.dtype)
        copies.append(pltpu.make_async_copy(grad.at[at, :], out_ref.at[0, at, :], sems.at[i]))
        copies[-1].start()
    genc_out[...] = genc_in[...]
    gdec_out[...] = gdec_in[...]
    loss_out[0] = loss_in[0]
    for copy in copies:
        copy.wait()


def shards(tokens, route, blocks, weight, enc_bias, dec_bias):
    n_e = lax.axis_size("expert")
    n_l = lax.axis_size("latent")
    n_tok, width = tokens.shape
    list_len = blocks.shape[1]
    latents = weight.shape[2]
    share = n_e * CAP
    count = n_l * share
    aug_width = -(-(width + LANES) // (PARTS * LANES)) * PARTS * LANES
    chunk = aug_width // PARTS
    fold = -(-(width + LANES) // (2 * LANES)) * LANES
    vmem = pl.BlockSpec(memory_space=pltpu.VMEM)
    dma = pltpu.SemaphoreType.DMA
    f32, bf16 = jnp.float32, jnp.bfloat16
    left, right, genc, gdec, loss = pl.pallas_call(
        functools.partial(step_kernel, n_e, n_l, n_tok, width, list_len),
        out_shape=(
            jax.ShapeDtypeStruct((2 * count, width), bf16),
            jax.ShapeDtypeStruct((2 * count, latents), bf16),
            jax.ShapeDtypeStruct((1, latents), f32),
            jax.ShapeDtypeStruct((width,), f32),
            jax.ShapeDtypeStruct((1,), f32),
        ),
        in_specs=[vmem, vmem, vmem, pl.BlockSpec(memory_space=pl.ANY), vmem, vmem],
        out_specs=[pl.BlockSpec(memory_space=pl.ANY)] * 2 + [vmem] * 2 + [pl.BlockSpec(memory_space=pltpu.SMEM)],
        scratch_shapes=[
            pltpu.VMEM((2 * count, width), bf16),
            pltpu.VMEM((2 * count, latents), bf16),
            pltpu.VMEM((width, latents), bf16),
            pltpu.VMEM((n_tok, aug_width), f32),
            pltpu.VMEM((n_e, PACK, chunk), bf16),
            pltpu.VMEM((n_e, PACK, chunk), bf16),
            pltpu.VMEM((n_l, 2 * share, fold), bf16),
            pltpu.VMEM((count, 2 * fold), f32),
            pltpu.VMEM((count, width), bf16),
            pltpu.VMEM((count, latents), f32),
            pltpu.VMEM((count, width), f32),
            pltpu.VMEM((2, n_l, 2 * share, width // 4), bf16),
            pltpu.VMEM((2, n_l, 2 * share, width // 4), bf16),
            pltpu.VMEM((2, n_l, 2 * share, width // 4), bf16),
            pltpu.VMEM((count, width // 2), f32),
            pltpu.VMEM((count, latents), f32),
            pltpu.VMEM((2, n_e, 1, width // 2 + LANES), f32),
            pltpu.VMEM((2, n_l, 1, width // 2 + LANES), f32),
            dma, dma((2,)),
            dma((n_e,)), dma((n_e,)),
            dma((2 * n_l,)), dma((n_l,)),
            dma((2, n_l)), dma((2, n_l)),
            dma((2, n_l)), dma((2, n_l)),
            dma((2, n_e)), dma((2, n_e)),
            dma((2, n_l)), dma((2, n_l)),
        ],
        compiler_params=pltpu.CompilerParams(
            collective_id=0, has_side_effects=True, vmem_limit_bytes=56 << 20),
        name="sae_step",
    )(tokens, route.reshape(1, n_tok), blocks, weight, enc_bias, dec_bias)
    small = [vmem, vmem, pl.BlockSpec(memory_space=pltpu.SMEM)]
    grad, genc, gdec, loss = pl.pallas_call(
        grad_kernel,
        out_shape=(
            jax.ShapeDtypeStruct((1, width, latents), bf16),
            jax.ShapeDtypeStruct((1, latents), f32),
            jax.ShapeDtypeStruct((width,), f32),
            jax.ShapeDtypeStruct((1,), f32),
        ),
        in_specs=[vmem, vmem] + small,
        out_specs=[pl.BlockSpec(memory_space=pl.ANY)] + small,
        scratch_shapes=[pltpu.VMEM((width, latents), bf16), dma((width // TILE,))],
        compiler_params=pltpu.CompilerParams(vmem_limit_bytes=56 << 20),
        name="grad_weight",
    )(left, right, genc, gdec, loss)
    return grad, genc, gdec, loss[0]


def solution(mesh):
    return jax.shard_map(
        shards,
        mesh=mesh,
        in_specs=(
            P(("expert", "latent"), None),
            P(("expert", "latent"), None),
            P(("expert", "latent"), None),
            P("expert", None, "latent"),
            P("expert", "latent"),
            P(),
        ),
        out_specs=(P("expert", None, "latent"), P("expert", "latent"), P(), P()),
        check_vma=False,
    )
```

```python
import functools
import jax
import jax.numpy as jnp
from jax import lax
from jax.experimental import pallas as pl
from jax.experimental.pallas import tpu as pltpu
from jax.sharding import PartitionSpec as P

BLK = 128
CAP = 2
PACK = 16
PARTS = PACK // CAP
LANES = 128
TILE = 256
MESH = pl.DeviceIdType.MESH
ALONG_LAST = (((1,), (1,)), ((), ()))
ALONG_FIRST = (((0,), (0,)), ((), ()))


def step_kernel(
    n_e, n_l, n_tok, width, list_len,
    tok_ref, route_ref, blocks_ref, w_hbm, encb_ref, decb_ref,
    left_out, right_out, genc_ref, gdec_ref, loss_ref,
    left_ref, right_ref, w_ref, aug, pack, mine, gathered, rows, shifted, gate, part, rs_send, rs_recv, ag_recv, err, acc, vec_e, vec_l,
    w_sem, out_sem, s1, r1, s2, r2, s3, r3, s4, r4, s5, r5, s6, r6,
):
    me_e = lax.axis_index("expert")
    me_l = lax.axis_index("latent")
    share = n_e * CAP
    count = n_l * share
    half = width // 2
    quarter = half // 2
    chunk = aug.shape[1] // PARTS
    latents = w_ref.shape[1]
    few = count <= LANES
    wide = latents if few else TILE
    deep = half if few else TILE

    def to_expert(src, dst, ssem, rsem, peer, slot):
        return pltpu.make_async_remote_copy(
            src_ref=src, dst_ref=dst, send_sem=ssem.at[peer], recv_sem=rsem.at[slot],
            device_id=(peer, me_l), device_id_type=MESH)

    def to_latent(src, dst, ssem, rsem, peer, slot):
        return pltpu.make_async_remote_copy(
            src_ref=src, dst_ref=dst, send_sem=ssem.at[peer], recv_sem=rsem.at[slot],
            device_id=(me_e, peer), device_id_type=MESH)

    def steps(n):
        if n == 1:
            return lambda body: body(0)
        return pl.loop(0, n)

    def peers(me, n):
        return [lax.rem(me + k, n) for k in range(1, n)]

    barrier = pltpu.get_barrier_semaphore()
    for p in peers(me_e, n_e):
        pl.semaphore_signal(barrier, inc=1, device_id=(p, me_l), device_id_type=MESH)
    for p in peers(me_l, n_l):
        pl.semaphore_signal(barrier, inc=1, device_id=(me_e, p), device_id_type=MESH)

    w_copy = pltpu.make_async_copy(w_hbm.at[0], w_ref, w_sem)
    w_copy.start()

    aug[...] = jnp.zeros_like(aug)
    aug[:, :width] = tok_ref[...].astype(jnp.float32)
    aug[:, width:width + list_len] = (blocks_ref[...] + 1).astype(jnp.float32)
    route = jnp.broadcast_to(route_ref[...], (8, n_tok))
    one_hot = (route == lax.broadcasted_iota(jnp.int32, (8, n_tok), 0)).astype(jnp.float32)
    before = (lax.broadcasted_iota(jnp.int32, (n_tok, n_tok), 0)
              < lax.broadcasted_iota(jnp.int32, (n_tok, n_tok), 1)).astype(jnp.float32)
    earlier = jnp.sum(jnp.dot(one_hot, before, preferred_element_type=jnp.float32) * one_hot, axis=0, keepdims=True)
    target = (route.astype(jnp.float32) * CAP + earlier).astype(jnp.bfloat16)
    repeat = (lax.broadcasted_iota(jnp.int32, (n_tok, PARTS * n_tok), 0)
              == (lax.broadcasted_iota(jnp.int32, (n_tok, PARTS * n_tok), 1) & (n_tok - 1))).astype(jnp.bfloat16)
    target = jnp.dot(target, repeat, preferred_element_type=jnp.float32)[:1]
    stacked = jnp.concatenate([aug[:, c * chunk:(c + 1) * chunk] for c in range(PARTS)], axis=0).astype(jnp.bfloat16)
    shape = (n_e * PACK, PARTS * n_tok)
    row = lax.broadcasted_iota(jnp.int32, shape, 0)
    col = lax.broadcasted_iota(jnp.int32, shape, 1)
    place = (row >> 4) * CAP + (row & 1)
    hit = (target == place.astype(jnp.float32)) & (col // n_tok == ((row >> 1) & (PARTS - 1)))
    packed = jnp.dot(hit.astype(jnp.bfloat16), stacked, preferred_element_type=jnp.float32)
    pack[...] = packed.astype(jnp.bfloat16).reshape(pack.shape)

    pl.semaphore_wait(barrier, (n_e - 1) + (n_l - 1))
    for p in peers(me_e, n_e):
        to_expert(pack.at[p], mine.at[me_e], s1, r1, p, me_e).start()
    mine[me_e] = pack[me_e]
    for p in peers(me_e, n_e):
        to_expert(pack.at[p], mine.at[p], s1, r1, p, p).wait_recv()
    shape = (n_e * PACK, n_e * PACK)
    row = lax.broadcasted_iota(jnp.int32, shape, 0)
    col = lax.broadcasted_iota(jnp.int32, shape, 1)
    unpack = (row == ((col >> 1) & (PARTS - 1)) * share + (col >> 4) * CAP + (col & 1)).astype(jnp.bfloat16)
    flat = jnp.dot(unpack, mine[...].reshape(n_e * PACK, chunk), preferred_element_type=jnp.float32)
    flat = jnp.concatenate([flat[c * share:(c + 1) * share] for c in range(PARTS)], axis=1)
    fold = gathered.shape[2]
    gathered[me_l] = jnp.concatenate([flat[:, :fold], flat[:, fold:2 * fold]], axis=0).astype(jnp.bfloat16)
    for p in peers(me_l, n_l):
        to_latent(gathered.at[me_l], gathered.at[me_l], s2, r2, p, me_l).start()

    def place_rows(source):
        block = gathered[source].astype(jnp.float32)
        at = pl.ds(pl.multiple_of(source * share, 8), share)
        rows[at, :fold] = block[:share]
        rows[at, fold:] = block[share:]

    place_rows(me_l)

    @pl.loop(1, n_l)
    def _(k):
        p = lax.rem(me_l + k, n_l)
        to_latent(gathered.at[p], gathered.at[p], s2, r2, p, p).wait_recv()
        place_rows(p)

    decb = decb_ref[...].reshape(1, width)
    bf = (rows[:, :width] - decb).astype(jnp.bfloat16)
    shifted[...] = bf
    left_ref[:count, :] = bf
    lists = rows[:, width:width + LANES]
    first_block = me_l * (latents // BLK)
    for b in range(latents // BLK):
        number = (first_block + b + 1).astype(jnp.float32)
        found = jnp.max((lists == number).astype(jnp.float32), axis=1, keepdims=True)
        gate[:, b * BLK:(b + 1) * BLK] = jnp.broadcast_to(found, (count, BLK))

    w_copy.wait()

    @steps(latents // wide)
    def _(j):
        at = pl.ds(j * wide if few else pl.multiple_of(j * wide, wide), wide)
        pre = jnp.dot(shifted[...], w_ref[:, at], preferred_element_type=jnp.float32) + encb_ref[:, at]
        mask = gate[:, at]
        right_ref[count:, at] = (jnp.maximum(pre, 0.0) * mask).astype(jnp.bfloat16)
        gate[:, at] = jnp.where(pre > 0.0, mask, 0.0)

    def folded(value):
        return jnp.concatenate([value[:, :quarter], value[:, quarter:]], axis=0)

    def unfolded(value):
        return jnp.concatenate([value[:share], value[share:]], axis=1)

    own = pl.ds(pl.multiple_of(me_l * share, 8), share)
    for h in range(2):
        @steps(half // deep)
        def _(j):
            at = pl.ds(h * half + j * deep if few else pl.multiple_of(h * half + j * deep, deep), deep)
            part[:, at] = lax.dot_general(
                right_ref[count:, :], w_ref[at, :], ALONG_LAST, preferred_element_type=jnp.float32)

        cols = slice(h * half, (h + 1) * half)

        @pl.loop(1, n_l)
        def _(k):
            p = lax.rem(me_l + k, n_l)
            rs_send[h, p] = folded(part[pl.ds(pl.multiple_of(p * share, 8), share), cols]).astype(jnp.bfloat16)
            to_latent(rs_send.at[h, p], rs_recv.at[h, me_l], s3.at[h], r3.at[h], p, me_l).start()

    valid = (rows[own, width:width + 1] > 0.5).astype(jnp.float32)
    loss = jnp.zeros((), jnp.float32)
    error_sum = []
    for h in range(2):
        cols = slice(h * half, (h + 1) * half)
        total = part[own, cols]
        for p in peers(me_l, n_l):
            to_latent(rs_send.at[h, p], rs_recv.at[h, p], s3.at[h], r3.at[h], p, p).wait_recv()
            total = total + unfolded(rs_recv[h, p].astype(jnp.float32))
        error = (total + decb[:, cols] - rows[own, cols]) * valid
        ag_recv[h, me_l] = folded(error).astype(jnp.bfloat16)
        for p in peers(me_l, n_l):
            to_latent(ag_recv.at[h, me_l], ag_recv.at[h, me_l], s4.at[h], r4.at[h], p, me_l).start()
        error_sum.append(jnp.sum(error, axis=0, keepdims=True))
        loss = loss + 0.5 * jnp.sum(error * error)
    error_sum = jnp.concatenate(error_sum, axis=1)

    for h in range(2):
        cols = slice(h * half, (h + 1) * half)

        def place_error(s):
            at = pl.ds(pl.multiple_of(s * share, 8), share)
            err[at, :] = unfolded(ag_recv[h, s].astype(jnp.float32))

        place_error(me_l)

        @pl.loop(1, n_l)
        def _(k):
            p = lax.rem(me_l + k, n_l)
            to_latent(ag_recv.at[h, p], ag_recv.at[h, p], s4.at[h], r4.at[h], p, p).wait_recv()
            place_error(p)

        left_ref[count:, cols] = err[...].astype(jnp.bfloat16)

        @steps(latents // wide)
        def _(j):
            at = pl.ds(j * wide if few else pl.multiple_of(j * wide, wide), wide)
            grad = jnp.dot(left_ref[count:, cols], w_ref[cols, at], preferred_element_type=jnp.float32)
            if h == 0:
                acc[:, at] = grad
            else:
                grad = (acc[:, at] + grad) * gate[:, at]
                right_ref[:count, at] = grad.astype(jnp.bfloat16)
                genc_ref[:, at] = jnp.sum(grad, axis=0, keepdims=True)

    stores = [pltpu.make_async_copy(left_ref, left_out, out_sem.at[0]),
              pltpu.make_async_copy(right_ref, right_out, out_sem.at[1])]
    for copy in stores:
        copy.start()

    column = jnp.broadcast_to(genc_ref[...], (8, latents)).astype(jnp.bfloat16)
    for h in range(2):
        for j in range(half // TILE):
            at = slice(h * half + j * TILE, h * half + (j + 1) * TILE)
            pulled = lax.dot_general(column, w_ref[at, :], ALONG_LAST, preferred_element_type=jnp.float32)
            vec_e[h, me_e, :, j * TILE:(j + 1) * TILE] = error_sum[:, at] - pulled[:1]
        vec_e[h, me_e, :, half:] = jnp.broadcast_to(loss.reshape(1, 1), (1, LANES))
        for p in peers(me_e, n_e):
            to_expert(vec_e.at[h, me_e], vec_e.at[h, me_e], s5.at[h], r5.at[h], p, me_e).start()
    for h in range(2):
        for p in peers(me_e, n_e):
            to_expert(vec_e.at[h, p], vec_e.at[h, p], s5.at[h], r5.at[h], p, p).wait_recv()
        vec = vec_e[h, 0]
        for s in range(1, n_e):
            vec = vec + vec_e[h, s]
        vec_l[h, me_l] = vec
        for p in peers(me_l, n_l):
            to_latent(vec_l.at[h, me_l], vec_l.at[h, me_l], s6.at[h], r6.at[h], p, me_l).start()
    ends = []
    for h in range(2):
        for p in peers(me_l, n_l):
            to_latent(vec_l.at[h, p], vec_l.at[h, p], s6.at[h], r6.at[h], p, p).wait_recv()
        vec = vec_l[h, 0]
        for s in range(1, n_l):
            vec = vec + vec_l[h, s]
        ends.append(vec)
    gdec_ref[...] = jnp.concatenate([ends[0][:, :half], ends[1][:, :half]], axis=1).reshape(width)
    loss_ref[0] = ends[0][0, half] * (1.0 / (n_tok * n_e * n_l))
    for copy in stores:
        copy.wait()

    for p in peers(me_e, n_e):
        to_expert(pack.at[p], mine.at[me_e], s1, r1, p, me_e).wait_send()
        for h in range(2):
            to_expert(vec_e.at[h, me_e], vec_e.at[h, me_e], s5.at[h], r5.at[h], p, me_e).wait_send()
    for p in peers(me_l, n_l):
        to_latent(gathered.at[me_l], gathered.at[me_l], s2, r2, p, me_l).wait_send()
    for h in range(2):
        for p in peers(me_l, n_l):
            to_latent(rs_send.at[h, p], rs_recv.at[h, me_l], s3.at[h], r3.at[h], p, me_l).wait_send()
            to_latent(vec_l.at[h, me_l], vec_l.at[h, me_l], s6.at[h], r6.at[h], p, me_l).wait_send()
            to_latent(ag_recv.at[h, me_l], ag_recv.at[h, me_l], s4.at[h], r4.at[h], p, me_l).wait_send()


def grad_kernel(left_ref, right_ref, genc_in, gdec_in, loss_in, out_ref, genc_out, gdec_out, loss_out, grad, sems):
    width = grad.shape[0]
    strip = width // sems.shape[0]
    copies = []
    for i in range(sems.shape[0]):
        at = slice(i * strip, (i + 1) * strip)
        grad[at, :] = lax.dot_general(
            left_ref[:, at], right_ref[...], ALONG_FIRST, preferred_element_type=jnp.float32).astype(grad.dtype)
        copies.append(pltpu.make_async_copy(grad.at[at, :], out_ref.at[0, at, :], sems.at[i]))
        copies[-1].start()
    genc_out[...] = genc_in[...]
    gdec_out[...] = gdec_in[...]
    loss_out[0] = loss_in[0]
    for copy in copies:
        copy.wait()


def shards(tokens, route, blocks, weight, enc_bias, dec_bias):
    n_e = lax.axis_size("expert")
    n_l = lax.axis_size("latent")
    n_tok, width = tokens.shape
    list_len = blocks.shape[1]
    latents = weight.shape[2]
    share = n_e * CAP
    count = n_l * share
    aug_width = -(-(width + LANES) // (PARTS * LANES)) * PARTS * LANES
    chunk = aug_width // PARTS
    fold = -(-(width + LANES) // (2 * LANES)) * LANES
    vmem = pl.BlockSpec(memory_space=pltpu.VMEM)
    dma = pltpu.SemaphoreType.DMA
    f32, bf16 = jnp.float32, jnp.bfloat16
    left, right, genc, gdec, loss = pl.pallas_call(
        functools.partial(step_kernel, n_e, n_l, n_tok, width, list_len),
        out_shape=(
            jax.ShapeDtypeStruct((2 * count, width), bf16),
            jax.ShapeDtypeStruct((2 * count, latents), bf16),
            jax.ShapeDtypeStruct((1, latents), f32),
            jax.ShapeDtypeStruct((width,), f32),
            jax.ShapeDtypeStruct((1,), f32),
        ),
        in_specs=[vmem, vmem, vmem, pl.BlockSpec(memory_space=pl.ANY), vmem, vmem],
        out_specs=[pl.BlockSpec(memory_space=pl.ANY)] * 2 + [vmem] * 2 + [pl.BlockSpec(memory_space=pltpu.SMEM)],
        scratch_shapes=[
            pltpu.VMEM((2 * count, width), bf16),
            pltpu.VMEM((2 * count, latents), bf16),
            pltpu.VMEM((width, latents), bf16),
            pltpu.VMEM((n_tok, aug_width), f32),
            pltpu.VMEM((n_e, PACK, chunk), bf16),
            pltpu.VMEM((n_e, PACK, chunk), bf16),
            pltpu.VMEM((n_l, 2 * share, fold), bf16),
            pltpu.VMEM((count, 2 * fold), f32),
            pltpu.VMEM((count, width), bf16),
            pltpu.VMEM((count, latents), f32),
            pltpu.VMEM((count, width), f32),
            pltpu.VMEM((2, n_l, 2 * share, width // 4), bf16),
            pltpu.VMEM((2, n_l, 2 * share, width // 4), bf16),
            pltpu.VMEM((2, n_l, 2 * share, width // 4), bf16),
            pltpu.VMEM((count, width // 2), f32),
            pltpu.VMEM((count, latents), f32),
            pltpu.VMEM((2, n_e, 1, width // 2 + LANES), f32),
            pltpu.VMEM((2, n_l, 1, width // 2 + LANES), f32),
            dma, dma((2,)),
            dma((n_e,)), dma((n_e,)),
            dma((n_l,)), dma((n_l,)),
            dma((2, n_l)), dma((2, n_l)),
            dma((2, n_l)), dma((2, n_l)),
            dma((2, n_e)), dma((2, n_e)),
            dma((2, n_l)), dma((2, n_l)),
        ],
        compiler_params=pltpu.CompilerParams(
            collective_id=0, has_side_effects=True, vmem_limit_bytes=56 << 20),
        name="sae_step",
    )(tokens, route.reshape(1, n_tok), blocks, weight, enc_bias, dec_bias)
    small = [vmem, vmem, pl.BlockSpec(memory_space=pltpu.SMEM)]
    grad, genc, gdec, loss = pl.pallas_call(
        grad_kernel,
        out_shape=(
            jax.ShapeDtypeStruct((1, width, latents), bf16),
            jax.ShapeDtypeStruct((1, latents), f32),
            jax.ShapeDtypeStruct((width,), f32),
            jax.ShapeDtypeStruct((1,), f32),
        ),
        in_specs=[vmem, vmem] + small,
        out_specs=[pl.BlockSpec(memory_space=pl.ANY)] + small,
        scratch_shapes=[pltpu.VMEM((width, latents), bf16), dma((width // TILE,))],
        compiler_params=pltpu.CompilerParams(vmem_limit_bytes=56 << 20),
        name="grad_weight",
    )(left, right, genc, gdec, loss)
    return grad, genc, gdec, loss[0]


def solution(mesh):
    return jax.shard_map(
        shards,
        mesh=mesh,
        in_specs=(
            P(("expert", "latent"), None),
            P(("expert", "latent"), None),
            P(("expert", "latent"), None),
            P("expert", None, "latent"),
            P("expert", "latent"),
            P(),
        ),
        out_specs=(P("expert", None, "latent"), P("expert", "latent"), P(), P()),
        check_vma=False,
    )
```
